32 devices in a mesh: dp: 4 (over y, core), pipe: 4 (over z), tensor: 2 (over x).
Axes of the slice: x: 2, y: 2, z: 4, core: 2. Of those that a mesh axis runs over, the one named last changes fastest.
Arguments:
- inputs: bfloat16 [4, 1024, 8192], P('pipe', 'dp', 'tensor'), may hold values from -900 to 900
- norm_gain: float32 [4, 8192], P('pipe', 'tensor'), may hold values from 0.1 to 1.9
- value_weight: bfloat16 [4, 1024, 8192], P('pipe', None, 'tensor'), may hold values from -1 to 1
- value_cotangent: bfloat16 [4, 1024, 1024], P('pipe', 'dp'), may hold values from -6 to 6
- upper_grad: bfloat16 [4, 1024, 8192], P('pipe', 'dp', 'tensor'), may hold values from -3 to 3
Outputs:
- input_grad: bfloat16 [4, 1024, 8192], P('pipe', 'dp', 'tensor')
- weight_grad: float32 [4, 1024, 8192], P('pipe', 'dp', 'tensor')
- gain_grad: float32 [4, 8192], P('pipe', 'tensor')
The draws below stay inside these ranges and needn't reach their ends.
All inputs are finite; a program needn't handle non-finite values.
Results may differ from the reference program's by a relative error of at most 0.014.
Values may be sent and summed in bfloat16 or wider, within the bound.
No kernel may reach another device: no remote copies, remote signals or barrier semaphores. Data moves between devices by JAX's collectives and lax.ppermute only.
A program may use at most 64 MiB of HBM per device.

```python
import math
import jax
import jax.numpy as jnp
from jax import lax

D = 8192
KV = 1024
TOK_DEV = 256
TOKENS = 1024
SECTIONS = 4


def feature_profile(key):
    return jnp.clip(jax.random.normal(jax.random.fold_in(key, 4242), (SECTIONS, 1, D), jnp.float32), -3.0, 3.0)


def draw_inputs(key, part):
    first, second, third = jax.random.split(key, 3)
    profile = feature_profile(key)
    row_scale = jnp.exp(jax.random.uniform(second, (SECTIONS, TOKENS, 1), jnp.float32) * math.log(10.0))
    position = jnp.arange(D).astype(jnp.float32) / D
    jitter = jnp.exp(jax.random.uniform(third, (SECTIONS, 1, D), jnp.float32, -math.log(1.25), math.log(1.25)))
    col_scale = jnp.exp(position * math.log(10.0))[None, None, :] * jitter
    base = jnp.clip(jax.random.normal(first, (SECTIONS, TOKENS, D), jnp.float32), -4.0, 4.0)
    return ((base + profile) * row_scale * col_scale).astype(jnp.bfloat16)


def draw_value_weight(key, part):
    profile = feature_profile(key)
    first, second = jax.random.split(jax.random.fold_in(key, 77), 2)
    noise = jnp.clip(jax.random.normal(first, (SECTIONS, KV, D), jnp.float32), -4.0, 4.0)
    loads = jnp.clip(jax.random.normal(second, (SECTIONS, KV, 1), jnp.float32), -3.0, 3.0)
    drawn = (noise + loads * profile) / math.sqrt(KV)
    return jnp.clip(drawn, -1.0, 1.0).astype(jnp.bfloat16)


def with_spikes(values, rng, source, target, shards_of, factor):
    owner, partner = [(jnp.arange(values.shape[dim]) // (values.shape[dim] // shards_of)).reshape([-1 if axis == dim else 1 for axis in range(values.ndim)]) for dim in (source, target)]
    chosen = jax.random.permutation(rng, shards_of)[partner]
    strong = (owner == chosen) | (owner == (partner + shards_of // 2) % shards_of)
    return jnp.where(strong, factor * values, values)


def level_of(stream_key, shape, shards, least, largest):
    loudness, own = 1.0, jax.random.fold_in(stream_key, 6)
    for axis_at, blocks in shards:
        heights = jnp.exp(jax.random.uniform(jax.random.fold_in(own, axis_at), (blocks,), jnp.float32, least / len(shards), largest / len(shards)))
        loudness = loudness * jnp.repeat(heights, shape[axis_at] // blocks).reshape([-1 if axis == axis_at else 1 for axis in range(len(shape))])
    return loudness


def normal_values(stream_key, dims, spread, reach, cuts=(), dtype=jnp.bfloat16):
    entries = spread * jax.random.normal(stream_key, dims, jnp.float32)
    if cuts:
        entries = entries * level_of(stream_key, dims, cuts, -0.22, 0.18)
    return jnp.clip(entries, -reach, reach).astype(dtype)


def gaussian_with(rng, dims, deviation, reach, pieces, heavy, kind=jnp.bfloat16):
    values = deviation * jax.random.normal(rng, dims, jnp.float32)
    if pieces:
        values = values * level_of(rng, dims, pieces, -0.22, 0.18)
    return jnp.clip(with_spikes(values, jax.random.fold_in(rng, 3), *heavy), -reach, reach).astype(kind)


def setup_inputs(seed: int = 0) -> dict:
    keys = jax.random.split(jax.random.key(seed), 6)
    inputs = draw_inputs(jax.random.fold_in(keys[5], 71), 0)
    norm_gain = jnp.clip(1.0 + 0.18 * jax.random.normal(keys[1], (SECTIONS, D), jnp.float32), 0.1, 1.9)
    value_weight = draw_value_weight(jax.random.fold_in(keys[5], 71), 0)
    value_cotangent = gaussian_with(keys[3], (SECTIONS, TOKENS, KV), 1.0, 6.0, ((0, 4), (1, 4)), (1, 2, 4, 2.0))
    upper_grad = normal_values(keys[4], (SECTIONS, TOKENS, D), 0.5, 3.0, ((0, 4), (1, 4), (2, 2)))
    return {"inputs": inputs, "norm_gain": norm_gain, "value_weight": value_weight, "value_cotangent": value_cotangent, "upper_grad": upper_grad}


def section_backward(carry, section):
    inputs, norm_gain, value_weight, value_cotangent, upper_grad = carry
    input_rows = inputs[section].astype(jnp.float32)
    gain_row = norm_gain[section]
    weight_rows = value_weight[section]
    cotangent = value_cotangent[section]
    nxt = jnp.minimum(section + 1, SECTIONS - 1).astype(jnp.int32)
    keep_upper = (section + 1 < SECTIONS).astype(jnp.float32)
    upper_rows = upper_grad[nxt].astype(jnp.float32) * keep_upper
    grad_scale = 1.0 / jnp.sqrt(jnp.float32(TOKENS))
    inverse_rms = lax.rsqrt(lax.optimization_barrier(jnp.mean(input_rows * input_rows, axis=1, keepdims=True)) + 1e-05)
    normed = input_rows * inverse_rms
    hidden = (normed * gain_row).astype(jnp.bfloat16)
    hidden_grad = jnp.dot(cotangent, weight_rows, preferred_element_type=jnp.float32)
    gain_grad = lax.optimization_barrier(jnp.sum(hidden_grad * normed, axis=0)) * grad_scale
    center = lax.optimization_barrier(jnp.mean(gain_row * hidden_grad * normed, axis=1, keepdims=True))
    local_grad = inverse_rms * (gain_row * hidden_grad - normed * center)
    input_grad = (local_grad + upper_rows).astype(jnp.bfloat16)
    blocks = TOKENS // TOK_DEV
    cot_blocks = cotangent.reshape(blocks, TOK_DEV, KV)
    hid_blocks = hidden.reshape(blocks, TOK_DEV, D)

    def add_block(total, pair):
        cot_block, hid_block = pair
        partial_value = lax.dot_general(cot_block, hid_block, (((0,), (0,)), ((), ())), preferred_element_type=jnp.float32) * grad_scale
        partial_value = lax.optimization_barrier(partial_value.astype(jnp.bfloat16))
        return (total + partial_value.astype(jnp.float32), None)
    weight_grad, unused = lax.scan(add_block, jnp.zeros((KV, D), jnp.float32), (cot_blocks, hid_blocks))
    return (carry, (input_grad, weight_grad, gain_grad))

def reference(inputs, norm_gain, value_weight, value_cotangent, upper_grad):
    carry = (inputs, norm_gain, value_weight, value_cotangent, upper_grad)
    unused, outputs = lax.scan(section_backward, carry, jnp.arange(SECTIONS).astype(jnp.int32))
    return (outputs[0], outputs[1], outputs[2])
```

```python
import functools

import jax
import jax.numpy as jnp
from jax import lax
from jax.experimental import pallas as pl
from jax.experimental.pallas import tpu as pltpu
from jax.sharding import PartitionSpec as P

D = 8192
EPS = 1e-05
Y_CHUNKS = 4
Z_CHUNKS = 4
MIB = 1 << 20


def after(value, *others):
    return lax.optimization_barrier((value,) + others)[0]


def shifted(array, axis, by):
    count = lax.axis_size(axis)
    return lax.ppermute(array, axis, [(i, (i + by) % count) for i in range(count)])


def sum_over(array, axis):
    total = array
    for by in range(1, lax.axis_size(axis)):
        total = total + shifted(array, axis, by)
    return total


class Replicas:
    def __init__(self, axis):
        self.axis = axis
        self.count = lax.axis_size(axis)
        self.width = 2 if self.count % 2 == 0 else 1
        self.groups = self.count // self.width

    def to(self, index, high, low):
        return (index // self.width + high) % self.groups * self.width + (index % self.width + low) % self.width

    def send(self, array, high, low):
        return lax.ppermute(array, self.axis, [(i, self.to(i, high, low)) for i in range(self.count)])


def square_sum_kernel(x_ref, out_ref):
    x = x_ref[...].astype(jnp.float32)
    out_ref[...] = jnp.sum(x * x, axis=1, keepdims=True)


def weight_kernel(sources, *refs):
    cots, blocks = refs[:sources], refs[sources : 2 * sources]
    gain_ref, out_ref = refs[2 * sources], refs[-1]
    total = None
    for cot, block in zip(cots, blocks):
        term = lax.dot_general(
            cot[...], block[...], (((0,), (0,)), ((), ())), preferred_element_type=jnp.float32
        )
        total = term if total is None else total + term
    out_ref[...] = total * gain_ref[...]


def weight_chunk(cots, own, received, gain_row, out, chunk, chunks):
    tokens, features = own.shape
    rows = cots[0].shape[1]
    width = features // chunks
    tile = min(width, 512)
    steps = width // tile
    first = chunk * steps
    sources = len(cots)
    whole = lambda c: (0, 0)
    placed = lambda c: (0, first + c)
    here = lambda c: (0, c)
    in_specs = [pl.BlockSpec((tokens, rows), whole)] * sources
    in_specs += [pl.BlockSpec((tokens, tile), placed)]
    in_specs += [pl.BlockSpec((tokens, tile), here)] * (sources - 1)
    in_specs += [pl.BlockSpec((1, tile), placed)]
    args = [*cots, own, *received, gain_row]
    aliases = {}
    if out is not None:
        in_specs.append(pl.BlockSpec(memory_space=pl.ANY))
        aliases = {len(args): 0}
        args.append(out)
    return pl.pallas_call(
        functools.partial(weight_kernel, sources),
        grid=(steps,),
        in_specs=in_specs,
        out_specs=pl.BlockSpec((rows, tile), placed),
        out_shape=jax.ShapeDtypeStruct((rows, features), jnp.float32),
        input_output_aliases=aliases,
        compiler_params=pltpu.CompilerParams(vmem_limit_bytes=32 * MIB),
        cost_estimate=pl.CostEstimate(
            flops=2 * sources * tokens * rows * width,
            bytes_accessed=2 * sources * tokens * (rows + width) + 4 * rows * width,
            transcendentals=0,
        ),
    )(*args)


def per_device(inputs, norm_gain, value_weight, value_cotangent, upper_grad):
    replicas = Replicas("dp")
    sections = lax.axis_size("pipe")
    x = inputs[0]
    tokens, features = x.shape
    gain_row = norm_gain
    cotangent = value_cotangent[0]
    rows = cotangent.shape[1] // replicas.count
    grad_scale = float(tokens * replicas.count) ** (-0.5)
    me = lax.axis_index("dp")

    down = [(i, i - 1) for i in range(1, sections)]
    height = tokens // Z_CHUNKS
    width = features // Y_CHUNKS

    far = [(high, 0) for high in range(1, replicas.groups)]
    near = [(0, low) for low in range(1, replicas.width)]

    upper = []
    gate = None
    for c in range(Z_CHUNKS):
        part = upper_grad[0, c * height : (c + 1) * height]
        if c >= 2:
            part = after(part, upper[c - 2])
        upper.append(lax.ppermute(part, "pipe", down))

    gathered = []
    for c in range(Y_CHUNKS):
        part = x[:, c * width : (c + 1) * width]
        if c >= 2:
            part = after(part, *gathered[c - 2][: len(far)])
        gathered.append([replicas.send(part, high, low) for high, low in far])
    near_x = [replicas.send(x, high, low) for high, low in near]
    sources = [(0, 0)] + near + far + [(high, low) for high, _ in far for _, low in near]

    square_sum = sum_over(jnp.sum(jnp.square(x.astype(jnp.float32)), axis=1), "tensor")
    inverse_rms = lax.rsqrt(square_sum / D + EPS)[:, None]

    scaled = (cotangent.astype(jnp.float32) * (inverse_rms * grad_scale)).astype(jnp.bfloat16)
    cots = []
    for high, low in sources:
        part = lax.dynamic_slice_in_dim(scaled, replicas.to(me, high, low) * rows, rows, axis=1)
        cots.append(part if (high, low) == (0, 0) else replicas.send(part, high, low))

    normed = x.astype(jnp.float32) * inverse_rms
    hidden_grad = jnp.dot(cotangent, value_weight[0], preferred_element_type=jnp.float32)
    product = hidden_grad * normed
    center = (sum_over(jnp.sum(gain_row * product, axis=1), "tensor") / D)[:, None]
    gain_local = jnp.sum(product, axis=0, keepdims=True) * grad_scale
    for high_low in (near, far):
        total = gain_local
        for high, low in high_low:
            total = total + replicas.send(gain_local, high, low)
        gain_local = total
    gain_grad = gain_local
    local_grad = inverse_rms * (gain_row * hidden_grad - normed * center)
    received = jnp.concatenate(upper, axis=0).astype(jnp.float32)
    input_grad = (local_grad + received).astype(jnp.bfloat16)

    weight_grad = None
    for c in range(Y_CHUNKS):
        passed = [replicas.send(block, 0, low) for block in gathered[c] for _, low in near]
        near_part = [block[:, c * width : (c + 1) * width] for block in near_x]
        weight_grad = weight_chunk(
            cots, x, near_part + gathered[c] + passed, gain_row, weight_grad, c, Y_CHUNKS
        )
    return (input_grad[None], weight_grad[None], gain_grad)


def solution(mesh):
    return jax.shard_map(
        per_device,
        mesh=mesh,
        in_specs=(
            P("pipe", "dp", "tensor"),
            P("pipe", "tensor"),
            P("pipe", None, "tensor"),
            P("pipe", "dp", None),
            P("pipe", "dp", "tensor"),
        ),
        out_specs=(P("pipe", "dp", "tensor"), P("pipe", "dp", "tensor"), P("pipe", "tensor")),
        check_vma=False,
    )
```

```python
import functools

import jax
import jax.numpy as jnp
from jax import lax
from jax.experimental import pallas as pl
from jax.experimental.pallas import tpu as pltpu
from jax.sharding import PartitionSpec as P

D = 8192
EPS = 1e-05
Y_PARTS = (5, 3)
MIB = 1 << 20
PARAMS = pltpu.CompilerParams(vmem_limit_bytes=24 * MIB)


def after(value, *others):
    return lax.optimization_barrier((value,) + others)[0]


def spans(total, parts):
    unit = total // sum(parts)
    ends = [unit * sum(parts[: i + 1]) for i in range(len(parts))]
    return list(zip([0] + ends[:-1], [unit * p for p in parts]))


def tile_of(width, largest):
    tile = min(width, largest)
    while width % tile:
        tile //= 2
    return tile


def from_others(array, axis):
    count = lax.axis_size(axis)
    return [lax.ppermute(array, axis, [(i, (i + by) % count) for i in range(count)]) for by in range(1, count)]


class Replicas:
    def __init__(self, axis):
        self.axis = axis
        self.count = lax.axis_size(axis)
        self.width = 2 if self.count % 2 == 0 else 1
        self.groups = self.count // self.width
        self.high = lax.axis_index(axis) // self.width
        self.low = lax.axis_index(axis) % self.width

    def to(self, index, high, low):
        return (index // self.width + high) % self.groups * self.width + (index % self.width + low) % self.width

    def send(self, array, high, low):
        return lax.ppermute(array, self.axis, [(i, self.to(i, high, low)) for i in range(self.count)])


def lanes_to_row(sums):
    return jnp.sum(sums.T, axis=0, keepdims=True)


def row_to_column(row):
    return jnp.broadcast_to(row, (128, row.shape[1])).T[:, :1]


def fold_lanes(array):
    total = array[:, :128]
    for at in range(128, array.shape[1], 128):
        total = total + array[:, at : at + 128]
    return total


def grad_kernel(cot_ref, weight_ref, x_ref, gain_ref, hidden_grad_ref, sums_ref, squares, centers):
    step = pl.program_id(0)

    @pl.when(step == 0)
    def _():
        squares[...] = jnp.zeros_like(squares)
        centers[...] = jnp.zeros_like(centers)

    x = x_ref[...].astype(jnp.float32)
    hidden_grad = jnp.dot(cot_ref[...], weight_ref[...], preferred_element_type=jnp.float32)
    hidden_grad_ref[...] = hidden_grad
    squares[...] += fold_lanes(x * x)
    centers[...] += fold_lanes(gain_ref[...] * hidden_grad * x)

    @pl.when(step == pl.num_programs(0) - 1)
    def _():
        sums_ref[0:1] = lanes_to_row(squares[...])
        sums_ref[1:2] = lanes_to_row(centers[...])


def hidden_grad_and_sums(cotangent, weight, x, gain_row):
    tokens, features = x.shape
    tile = tile_of(features, 512)
    column = lambda c: (0, c)
    whole = lambda c: (0, 0)
    return pl.pallas_call(
        grad_kernel,
        grid=(features // tile,),
        in_specs=[
            pl.BlockSpec(cotangent.shape, whole),
            pl.BlockSpec((weight.shape[0], tile), column),
            pl.BlockSpec((tokens, tile), column),
            pl.BlockSpec((1, tile), column),
        ],
        out_specs=[pl.BlockSpec((tokens, tile), column), pl.BlockSpec((2, tokens), whole)],
        out_shape=[
            jax.ShapeDtypeStruct((tokens, features), jnp.float32),
            jax.ShapeDtypeStruct((2, tokens), jnp.float32),
        ],
        scratch_shapes=[pltpu.VMEM((tokens, 128), jnp.float32)] * 2,
        compiler_params=PARAMS,
        cost_estimate=pl.CostEstimate(
            flops=2 * tokens * features * weight.shape[0],
            bytes_accessed=2 * (weight.size + cotangent.size + x.size) + 4 * x.size,
            transcendentals=0,
        ),
    )(cotangent, weight, x, gain_row)


def local_kernel(scale, others, *refs):
    sums_refs = refs[: others + 1]
    cot_ref, x_ref, hidden_grad_ref, gain_ref = refs[others + 1 : others + 5]
    local_ref, gain_grad_ref, scaled_ref, inverse, factor = refs[others + 5 :]

    @pl.when(pl.program_id(0) == 0)
    def _():
        sums = sums_refs[0][...]
        for ref in sums_refs[1:]:
            sums = sums + ref[...]
        inverse_row = lax.rsqrt(sums[0:1] / D + EPS)
        center_row = inverse_row * sums[1:2] / D
        inverse[...] = row_to_column(inverse_row)
        factor[...] = row_to_column(inverse_row * center_row)
        scaled_ref[...] = (cot_ref[...].astype(jnp.float32) * (inverse[...] * scale)).astype(jnp.bfloat16)

    x = x_ref[...].astype(jnp.float32)
    hidden_grad = hidden_grad_ref[...]
    local_ref[...] = inverse[...] * (gain_ref[...] * hidden_grad - x * factor[...])
    gain_grad_ref[...] = jnp.sum(hidden_grad * x * inverse[...], axis=0, keepdims=True) * scale


def local_terms(sums, cotangent, x, hidden_grad, gain_row, scale):
    tokens, features = x.shape
    tile = tile_of(features, 512)
    column = lambda c: (0, c)
    whole = lambda c: (0, 0)
    return pl.pallas_call(
        functools.partial(local_kernel, scale, len(sums) - 1),
        grid=(features // tile,),
        in_specs=[pl.BlockSpec((2, tokens), whole)] * len(sums)
        + [
            pl.BlockSpec(cotangent.shape, whole),
            pl.BlockSpec((tokens, tile), column),
            pl.BlockSpec((tokens, tile), column),
            pl.BlockSpec((1, tile), column),
        ],
        out_specs=[
            pl.BlockSpec((tokens, tile), column),
            pl.BlockSpec((1, tile), column),
            pl.BlockSpec(cotangent.shape, whole),
        ],
        out_shape=[
            jax.ShapeDtypeStruct((tokens, features), jnp.float32),
            jax.ShapeDtypeStruct((1, features), jnp.float32),
            jax.ShapeDtypeStruct(cotangent.shape, jnp.bfloat16),
        ],
        scratch_shapes=[pltpu.VMEM((tokens, 1), jnp.float32)] * 2,
        compiler_params=PARAMS,
        cost_estimate=pl.CostEstimate(
            flops=8 * x.size, bytes_accessed=4 * cotangent.size + 10 * x.size, transcendentals=0
        ),
    )(*sums, cotangent, x, hidden_grad, gain_row)


def add_kernel(local_ref, received_ref, out_ref):
    out_ref[...] = (local_ref[...] + received_ref[...].astype(jnp.float32)).astype(out_ref.dtype)


def add_rows(local, received):
    height, features = received.shape
    tile = tile_of(height, 64)
    block = pl.BlockSpec((tile, features), lambda r: (r, 0))
    return pl.pallas_call(
        add_kernel,
        grid=(height // tile,),
        in_specs=[block, block],
        out_specs=block,
        out_shape=jax.ShapeDtypeStruct(local.shape, received.dtype),
        compiler_params=PARAMS,
        cost_estimate=pl.CostEstimate(flops=received.size, bytes_accessed=8 * received.size, transcendentals=0),
    )(local, received)


def weight_kernel(sources, *refs):
    cots, blocks = refs[:sources], refs[sources : 2 * sources]
    gain_ref, out_ref = refs[2 * sources], refs[-1]
    total = None
    for cot, block in zip(cots, blocks):
        term = lax.dot_general(
            cot[...], block[...], (((0,), (0,)), ((), ())), preferred_element_type=jnp.float32
        )
        total = term if total is None else total + term
    out_ref[...] = total * gain_ref[...]


def weight_columns(cots, held, received, gain_row, start, out):
    tokens, features = held[0].shape
    width = received[0].shape[1]
    rows = cots[0].shape[1]
    tile = tile_of(width, 512)
    first = start // tile
    sources = len(cots)
    whole = lambda c: (0, 0)
    placed = lambda c: (0, first + c)
    here = lambda c: (0, c)
    in_specs = [pl.BlockSpec((tokens, rows), whole)] * sources
    in_specs += [pl.BlockSpec((tokens, tile), placed)] * len(held)
    in_specs += [pl.BlockSpec((tokens, tile), here)] * len(received)
    in_specs += [pl.BlockSpec((1, tile), placed)]
    args, aliases = [*cots, *held, *received, gain_row], {}
    if out is not None:
        in_specs.append(pl.BlockSpec(memory_space=pl.ANY))
        aliases = {len(args): 0}
        args.append(out)
    return pl.pallas_call(
        functools.partial(weight_kernel, sources),
        grid=(width // tile,),
        in_specs=in_specs,
        out_specs=pl.BlockSpec((rows, tile), placed),
        out_shape=jax.ShapeDtypeStruct((rows, features), jnp.float32),
        input_output_aliases=aliases,
        compiler_params=PARAMS,
        cost_estimate=pl.CostEstimate(
            flops=2 * sources * tokens * rows * width,
            bytes_accessed=2 * sources * tokens * (rows + width) + 4 * rows * width,
            transcendentals=0,
        ),
    )(*args)


def per_device(inputs, norm_gain, value_weight, value_cotangent, upper_grad):
    replicas = Replicas("dp")
    sections = lax.axis_size("pipe")
    slices = lax.axis_size("tensor")
    x = inputs[0]
    tokens, features = x.shape
    gain_row = norm_gain
    cotangent = value_cotangent[0]
    rows = cotangent.shape[1] // replicas.count
    pair_rows = rows * replicas.width
    grad_scale = float(tokens * replicas.count) ** (-0.5)
    far = range(1, replicas.groups)
    near = range(1, replicas.width)

    down = [(i, i - 1) for i in range(1, sections)]
    upper = lax.ppermute(upper_grad[0], "pipe", down)

    columns = spans(features, Y_PARTS)

    def send_far(c, *gates):
        start, width = columns[c]
        part = (after(x, *gates) if gates else x)[:, start : start + width]
        return [replicas.send(part, high, 0) for high in far]

    far_x = [send_far(0)]
    hidden_grad, sums = hidden_grad_and_sums(cotangent, value_weight[0], x, gain_row)
    near_x = [replicas.send(after(x, sums), 0, low) for low in near]
    local, gain_grad, scaled = local_terms(
        [sums] + from_others(sums, "tensor"), cotangent, x, hidden_grad, gain_row, grad_scale
    )
    share = tokens // slices
    mine = lax.axis_index("tensor")
    own_share = lax.dynamic_slice_in_dim(scaled, mine * share, share, axis=0)
    sent = []
    for high in far:
        there = (replicas.high + high) % replicas.groups * pair_rows
        sent.append(lax.dynamic_slice_in_dim(own_share, there, pair_rows, axis=1))
    for c in range(1, len(columns)):
        far_x.append(send_far(c, *(far_x[c - 2] if c > 1 else sent)))
    pair_blocks = [lax.dynamic_slice_in_dim(scaled, replicas.high * pair_rows, pair_rows, axis=1)]
    for high, block in zip(far, sent):
        got = replicas.send(block, high, 0)
        shares = jnp.concatenate([got] + from_others(got, "tensor"), axis=0)
        pieces = [
            lax.dynamic_slice_in_dim(shares, (mine - at) % slices * share, share, axis=0) for at in range(slices)
        ]
        pair_blocks.append(jnp.concatenate(pieces, axis=0))
    pair_cot = jnp.concatenate(pair_blocks, axis=0)
    near_cots = [
        replicas.send(
            lax.dynamic_slice_in_dim(pair_cot, (replicas.low + low) % replicas.width * rows, rows, axis=1), 0, low
        )
        for low in near
    ]
    own_cot = lax.dynamic_slice_in_dim(pair_cot, replicas.low * rows, rows, axis=1)
    by_group = [own_cot] + near_cots
    blocks = [[cot[g * tokens : (g + 1) * tokens] for g in range(replicas.groups)] for cot in by_group]
    cots = [block[0] for block in blocks] + [block[high] for high in far for block in blocks]

    for others in ([(high, 0) for high in far], [(0, low) for low in near]):
        gain_grad = sum([replicas.send(gain_grad, *other) for other in others], gain_grad)

    input_grad = add_rows(local, upper)
    weight_grad = None
    for c, ((start, width), direct) in enumerate(zip(columns, far_x)):
        received = []
        for block in direct:
            gates = (input_grad, gain_grad, *near_cots) if c == len(columns) - 1 else (scaled,)
            handed = after(block, *gates)
            received += [block] + [replicas.send(handed, 0, low) for low in near]
        weight_grad = weight_columns(cots, [x] + near_x, received, gain_row, start, weight_grad)
    return (input_grad[None], weight_grad[None], gain_grad)


def solution(mesh):
    return jax.shard_map(
        per_device,
        mesh=mesh,
        in_specs=(
            P("pipe", "dp", "tensor"),
            P("pipe", "tensor"),
            P("pipe", None, "tensor"),
            P("pipe", "dp", None),
            P("pipe", "dp", "tensor"),
        ),
        out_specs=(P("pipe", "dp", "tensor"), P("pipe", "dp", "tensor"), P("pipe", "tensor")),
        check_vma=False,
    )
```

```python
import functools

import jax
import jax.numpy as jnp
from jax import lax
from jax.experimental import pallas as pl
from jax.experimental.pallas import tpu as pltpu
from jax.sharding import PartitionSpec as P

D = 8192
EPS = 1e-05
Y_PARTS = (1, 1)
MIB = 1 << 20
PARAMS = pltpu.CompilerParams(vmem_limit_bytes=24 * MIB)
STREAMED = pltpu.CompilerParams(vmem_limit_bytes=56 * MIB)


def after(value, *others):
    return lax.optimization_barrier((value,) + others)[0]


def spans(total, parts):
    unit = total // sum(parts)
    ends = [unit * sum(parts[: i + 1]) for i in range(len(parts))]
    return list(zip([0] + ends[:-1], [unit * p for p in parts]))


def tile_of(width, largest):
    tile = min(width, largest)
    while width % tile:
        tile //= 2
    return tile


def from_others(array, axis):
    count = lax.axis_size(axis)
    return [lax.ppermute(array, axis, [(i, (i + by) % count) for i in range(count)]) for by in range(1, count)]


class Replicas:
    def __init__(self, axis):
        self.axis = axis
        self.count = lax.axis_size(axis)
        self.width = 2 if self.count % 2 == 0 else 1
        self.groups = self.count // self.width

    def to(self, index, high, low):
        return (index // self.width + high) % self.groups * self.width + (index % self.width + low) % self.width

    def index(self, high, low):
        return self.to(lax.axis_index(self.axis), high, low)

    def send(self, array, high, low):
        return lax.ppermute(array, self.axis, [(i, self.to(i, high, low)) for i in range(self.count)])


def lanes_to_row(sums):
    return jnp.sum(sums.T, axis=0, keepdims=True)


def row_to_column(row):
    return jnp.broadcast_to(row, (128, row.shape[1])).T[:, :1]


def fold_lanes(array):
    total = array[:, :128]
    for at in range(128, array.shape[1], 128):
        total = total + array[:, at : at + 128]
    return total


def grad_kernel(cot_ref, weight_ref, x_ref, gain_ref, hidden_grad_ref, sums_ref, squares, centers):
    step = pl.program_id(0)

    @pl.when(step == 0)
    def _():
        squares[...] = jnp.zeros_like(squares)
        centers[...] = jnp.zeros_like(centers)

    x = x_ref[...].astype(jnp.float32)
    hidden_grad = jnp.dot(cot_ref[...], weight_ref[...], preferred_element_type=jnp.float32)
    hidden_grad_ref[...] = hidden_grad
    squares[...] += fold_lanes(x * x)
    centers[...] += fold_lanes(gain_ref[...] * hidden_grad * x)

    @pl.when(step == pl.num_programs(0) - 1)
    def _():
        sums_ref[0:1] = lanes_to_row(squares[...])
        sums_ref[1:2] = lanes_to_row(centers[...])


def hidden_grad_and_sums(cotangent, weight, x, gain_row):
    tokens, features = x.shape
    tile = tile_of(features, 512)
    column = lambda c: (0, c)
    whole = lambda c: (0, 0)
    return pl.pallas_call(
        grad_kernel,
        grid=(features // tile,),
        in_specs=[
            pl.BlockSpec(cotangent.shape, whole),
            pl.BlockSpec((weight.shape[0], tile), column),
            pl.BlockSpec((tokens, tile), column),
            pl.BlockSpec((1, tile), column),
        ],
        out_specs=[pl.BlockSpec((tokens, tile), column), pl.BlockSpec((2, tokens), whole)],
        out_shape=[
            jax.ShapeDtypeStruct((tokens, features), jnp.float32),
            jax.ShapeDtypeStruct((2, tokens), jnp.float32),
        ],
        scratch_shapes=[pltpu.VMEM((tokens, 128), jnp.float32)] * 2,
        compiler_params=STREAMED,
        cost_estimate=pl.CostEstimate(
            flops=2 * tokens * features * weight.shape[0],
            bytes_accessed=2 * (weight.size + cotangent.size + x.size) + 4 * x.size,
            transcendentals=0,
        ),
    )(cotangent, weight, x, gain_row)


def local_kernel(scale, others, *refs):
    sums_refs = refs[: others + 1]
    cot_ref, x_ref, hidden_grad_ref, gain_ref = refs[others + 1 : others + 5]
    local_ref, gain_grad_ref, scaled_ref, inverse, factor = refs[others + 5 :]

    @pl.when(pl.program_id(0) == 0)
    def _():
        sums = sums_refs[0][...]
        for ref in sums_refs[1:]:
            sums = sums + ref[...]
        inverse_row = lax.rsqrt(sums[0:1] / D + EPS)
        center_row = inverse_row * sums[1:2] / D
        inverse[...] = row_to_column(inverse_row)
        factor[...] = row_to_column(inverse_row * center_row)
        scaled_ref[...] = (cot_ref[...].astype(jnp.float32).T * (inverse_row * scale)).astype(jnp.bfloat16)

    x = x_ref[...].astype(jnp.float32)
    hidden_grad = hidden_grad_ref[...]
    local_ref[...] = inverse[...] * (gain_ref[...] * hidden_grad - x * factor[...])
    gain_grad_ref[...] = jnp.sum(hidden_grad * x * inverse[...], axis=0, keepdims=True) * scale


def local_terms(sums, cotangent, x, hidden_grad, gain_row, scale):
    tokens, features = x.shape
    tile = tile_of(features, 512)
    column = lambda c: (0, c)
    whole = lambda c: (0, 0)
    return pl.pallas_call(
        functools.partial(local_kernel, scale, len(sums) - 1),
        grid=(features // tile,),
        in_specs=[pl.BlockSpec((2, tokens), whole)] * len(sums)
        + [
            pl.BlockSpec(cotangent.shape, whole),
            pl.BlockSpec((tokens, tile), column),
            pl.BlockSpec((tokens, tile), column),
            pl.BlockSpec((1, tile), column),
        ],
        out_specs=[
            pl.BlockSpec((tokens, tile), column),
            pl.BlockSpec((1, tile), column),
            pl.BlockSpec(cotangent.shape[::-1], whole),
        ],
        out_shape=[
            jax.ShapeDtypeStruct((tokens, features), jnp.float32),
            jax.ShapeDtypeStruct((1, features), jnp.float32),
            jax.ShapeDtypeStruct(cotangent.shape[::-1], jnp.bfloat16),
        ],
        scratch_shapes=[pltpu.VMEM((tokens, 1), jnp.float32)] * 2,
        compiler_params=STREAMED,
        cost_estimate=pl.CostEstimate(
            flops=8 * x.size, bytes_accessed=4 * cotangent.size + 10 * x.size, transcendentals=0
        ),
    )(*sums, cotangent, x, hidden_grad, gain_row)


def split_kernel(columns, x_ref, *refs):
    parts, sems = refs[:-1], refs[-1]
    copies = [
        pltpu.make_async_copy(x_ref.at[:, start : start + width], part, sems.at[at])
        for at, ((start, width), part) in enumerate(zip(columns, parts))
    ]
    for copy in copies:
        copy.start()
    for copy in copies:
        copy.wait()


def split_columns(x, columns):
    return pl.pallas_call(
        functools.partial(split_kernel, columns),
        in_specs=[pl.BlockSpec(memory_space=pl.ANY)],
        out_specs=[pl.BlockSpec(memory_space=pl.ANY)] * len(columns),
        out_shape=[jax.ShapeDtypeStruct((x.shape[0], width), x.dtype) for _, width in columns],
        scratch_shapes=[pltpu.SemaphoreType.DMA((len(columns),))],
        cost_estimate=pl.CostEstimate(flops=0, bytes_accessed=4 * x.size, transcendentals=0),
    )(x)


def add_kernel(local_ref, received_ref, out_ref):
    out_ref[...] = (local_ref[...] + received_ref[...].astype(jnp.float32)).astype(out_ref.dtype)


def add_rows(local, received):
    height, features = received.shape
    tile = tile_of(height, 32)
    block = pl.BlockSpec((tile, features), lambda r: (r, 0))
    return pl.pallas_call(
        add_kernel,
        grid=(height // tile,),
        in_specs=[block, block],
        out_specs=block,
        out_shape=jax.ShapeDtypeStruct(local.shape, received.dtype),
        compiler_params=PARAMS,
        cost_estimate=pl.CostEstimate(flops=received.size, bytes_accessed=8 * received.size, transcendentals=0),
    )(local, received)


def weight_kernel(groups, *refs):
    scaled_refs, gain_ref, blocks, out_ref = refs[:groups], refs[groups], refs[groups + 1 :], refs[-1]
    tokens = blocks[0].shape[0]
    width = scaled_refs[0].shape[1] // tokens
    total = None
    for at in range(groups * width):
        scaled = scaled_refs[at // width][:, at % width * tokens : (at % width + 1) * tokens]
        term = jnp.dot(scaled, blocks[at][...], preferred_element_type=jnp.float32)
        total = term if total is None else total + term
    out_ref[...] = total * gain_ref[...]


def weight_columns(scaled, held, received, gain_row, start, out):
    tokens, features = held[0].shape
    width = received[0].shape[1]
    rows = scaled[0].shape[0]
    tile = tile_of(width, 512)
    first = start // tile
    whole = lambda c: (0, 0)
    placed = lambda c: (0, first + c)
    here = lambda c: (0, c)
    in_specs = [pl.BlockSpec(part.shape, whole) for part in scaled] + [pl.BlockSpec((1, tile), placed)]
    in_specs += [pl.BlockSpec((tokens, tile), placed)] * len(held)
    in_specs += [pl.BlockSpec((tokens, tile), here)] * len(received)
    args, aliases = [*scaled, gain_row, *held, *received], {}
    if out is not None:
        in_specs.append(pl.BlockSpec(memory_space=pl.ANY))
        aliases = {len(args): 0}
        args.append(out)
    sources = len(held) + len(received)
    return pl.pallas_call(
        functools.partial(weight_kernel, len(scaled)),
        grid=(width // tile,),
        in_specs=in_specs,
        out_specs=pl.BlockSpec((rows, tile), placed),
        out_shape=jax.ShapeDtypeStruct((rows, features), jnp.float32),
        input_output_aliases=aliases,
        compiler_params=PARAMS,
        cost_estimate=pl.CostEstimate(
            flops=2 * sources * tokens * rows * width,
            bytes_accessed=2 * sources * tokens * (rows + width) + 4 * rows * width,
            transcendentals=0,
        ),
    )(*args)


def per_device(inputs, norm_gain, value_weight, value_cotangent, upper_grad):
    replicas = Replicas("dp")
    sections = lax.axis_size("pipe")
    slices = lax.axis_size("tensor")
    x = inputs[0]
    tokens, features = x.shape
    gain_row = norm_gain
    cotangent = value_cotangent[0]
    rows = cotangent.shape[1] // replicas.count
    grad_scale = float(tokens * replicas.count) ** (-0.5)
    far = range(1, replicas.groups)
    near = range(1, replicas.width)

    columns = spans(features, Y_PARTS)
    parts = split_columns(x, columns)
    far_x = [[replicas.send(parts[0], high, 0) for high in far]]
    down = [(i, i - 1) for i in range(1, sections)]
    upper = lax.ppermute(after(upper_grad[0], parts[0]), "pipe", down)

    hidden_grad, sums = hidden_grad_and_sums(cotangent, value_weight[0], x, gain_row)
    near_x = [replicas.send(after(x, sums), 0, low) for low in near]
    local, gain_grad, scaled = local_terms(
        [sums] + from_others(sums, "tensor"), cotangent, x, hidden_grad, gain_row, grad_scale
    )

    by_core = scaled.reshape(replicas.count, rows, tokens)
    turn = replicas.width - 1
    rows_for = lambda high, low: lax.dynamic_index_in_dim(by_core, replicas.index(high, low), 0, False)
    pair = [[rows_for(high, turn if high else 0)] for high in range(replicas.groups)]
    for low in near:
        theirs = jnp.stack([rows_for(high, turn + low if high else low) for high in range(replicas.groups)])
        swapped = replicas.send(theirs, 0, low)
        for high in range(replicas.groups):
            pair[high].append(swapped[high])
    pair = [jnp.concatenate(blocks, axis=1) for blocks in pair]
    cots = [pair[0]]
    share = tokens * replicas.width // slices
    mine = lax.axis_index("tensor")
    got = [
        replicas.send(lax.dynamic_slice_in_dim(pair[high], mine * share, share, axis=1), high, turn) for high in far
    ]
    for block in got:
        shares = jnp.concatenate([block] + from_others(block, "tensor"), axis=1)
        pieces = [
            lax.dynamic_slice_in_dim(shares, (mine - at) % slices * share, share, axis=1) for at in range(slices)
        ]
        cots.append(jnp.concatenate(pieces, axis=1))
    gain_far = [replicas.send(gain_grad, high, turn) for high in far]
    gain_grad = sum(gain_far, gain_grad)

    far_x += [[replicas.send(after(part, *got, *gain_far), high, 0) for high in far] for part in parts[1:]]
    weight_grad = None
    for c, ((start, width), direct) in enumerate(zip(columns, far_x)):
        gates = got + gain_far
        if c == len(columns) - 1:
            input_grad = add_rows(local, upper)
            gated = after(gain_grad, input_grad)
            gain_grad = sum([replicas.send(gated, 0, low) for low in near], gated)
            gates = [gain_grad] + [w for w in [weight_grad] if w is not None]
        received = []
        for block in direct:
            handed = after(block, *gates) if gates else block
            received += [replicas.send(handed, 0, low) for low in near] + [block]
        weight_grad = weight_columns(cots, [x] + near_x, received, gain_row, start, weight_grad)
    return (input_grad[None], weight_grad[None], gain_grad)


def solution(mesh):
    return jax.shard_map(
        per_device,
        mesh=mesh,
        in_specs=(
            P("pipe", "dp", "tensor"),
            P("pipe", "tensor"),
            P("pipe", None, "tensor"),
            P("pipe", "dp", None),
            P("pipe", "dp", "tensor"),
        ),
        out_specs=(P("pipe", "dp", "tensor"), P("pipe", "dp", "tensor"), P("pipe", "tensor")),
        check_vma=False,
    )
```

```python
import functools

import jax
import jax.numpy as jnp
from jax import lax
from jax.experimental import pallas as pl
from jax.experimental.pallas import tpu as pltpu
from jax.sharding import PartitionSpec as P

D = 8192
EPS = 1e-05
Y_PARTS = (5, 3)
MIB = 1 << 20
PARAMS = pltpu.CompilerParams(vmem_limit_bytes=24 * MIB)


def after(value, *others):
    return lax.optimization_barrier((value,) + others)[0]


def spans(total, parts):
    unit = total // sum(parts)
    ends = [unit * sum(parts[: i + 1]) for i in range(len(parts))]
    return list(zip([0] + ends[:-1], [unit * p for p in parts]))


def tile_of(width, largest):
    tile = min(width, largest)
    while width % tile:
        tile //= 2
    return tile


def from_others(array, axis):
    count = lax.axis_size(axis)
    return [lax.ppermute(array, axis, [(i, (i + by) % count) for i in range(count)]) for by in range(1, count)]


class Replicas:
    def __init__(self, axis):
        self.axis = axis
        self.count = lax.axis_size(axis)
        self.width = 2 if self.count % 2 == 0 else 1
        self.groups = self.count // self.width

    def to(self, index, high, low):
        return (index // self.width + high) % self.groups * self.width + (index % self.width + low) % self.width

    def index(self, high, low):
        return self.to(lax.axis_index(self.axis), high, low)

    def send(self, array, high, low):
        return lax.ppermute(array, self.axis, [(i, self.to(i, high, low)) for i in range(self.count)])


def lanes_to_row(sums):
    return jnp.sum(sums.T, axis=0, keepdims=True)


def row_to_column(row):
    return jnp.broadcast_to(row, (128, row.shape[1])).T[:, :1]


def fold_lanes(array):
    total = array[:, :128]
    for at in range(128, array.shape[1], 128):
        total = total + array[:, at : at + 128]
    return total


def grad_kernel(cot_ref, weight_ref, x_ref, gain_ref, hidden_grad_ref, sums_ref, squares, centers):
    step = pl.program_id(0)

    @pl.when(step == 0)
    def _():
        squares[...] = jnp.zeros_like(squares)
        centers[...] = jnp.zeros_like(centers)

    x = x_ref[...].astype(jnp.float32)
    hidden_grad = jnp.dot(cot_ref[...], weight_ref[...], preferred_element_type=jnp.float32)
    hidden_grad_ref[...] = hidden_grad
    squares[...] += fold_lanes(x * x)
    centers[...] += fold_lanes(gain_ref[...] * hidden_grad * x)

    @pl.when(step == pl.num_programs(0) - 1)
    def _():
        sums_ref[0:1] = lanes_to_row(squares[...])
        sums_ref[1:2] = lanes_to_row(centers[...])


def hidden_grad_and_sums(cotangent, weight, x, gain_row):
    tokens, features = x.shape
    tile = tile_of(features, 512)
    column = lambda c: (0, c)
    whole = lambda c: (0, 0)
    return pl.pallas_call(
        grad_kernel,
        grid=(features // tile,),
        in_specs=[
            pl.BlockSpec(cotangent.shape, whole),
            pl.BlockSpec((weight.shape[0], tile), column),
            pl.BlockSpec((tokens, tile), column),
            pl.BlockSpec((1, tile), column),
        ],
        out_specs=[pl.BlockSpec((tokens, tile), column), pl.BlockSpec((2, tokens), whole)],
        out_shape=[
            jax.ShapeDtypeStruct((tokens, features), jnp.float32),
            jax.ShapeDtypeStruct((2, tokens), jnp.float32),
        ],
        scratch_shapes=[pltpu.VMEM((tokens, 128), jnp.float32)] * 2,
        compiler_params=PARAMS,
        cost_estimate=pl.CostEstimate(
            flops=2 * tokens * features * weight.shape[0],
            bytes_accessed=2 * (weight.size + cotangent.size + x.size) + 4 * x.size,
            transcendentals=0,
        ),
    )(cotangent, weight, x, gain_row)


def local_kernel(scale, others, *refs):
    sums_refs = refs[: others + 1]
    cot_ref, x_ref, hidden_grad_ref, gain_ref = refs[others + 1 : others + 5]
    local_ref, gain_grad_ref, scaled_ref, inverse, factor = refs[others + 5 :]

    @pl.when(pl.program_id(0) == 0)
    def _():
        sums = sums_refs[0][...]
        for ref in sums_refs[1:]:
            sums = sums + ref[...]
        inverse_row = lax.rsqrt(sums[0:1] / D + EPS)
        center_row = inverse_row * sums[1:2] / D
        inverse[...] = row_to_column(inverse_row)
        factor[...] = row_to_column(inverse_row * center_row)
        scaled_ref[...] = (cot_ref[...].astype(jnp.float32).T * (inverse_row * scale)).astype(jnp.bfloat16)

    x = x_ref[...].astype(jnp.float32)
    hidden_grad = hidden_grad_ref[...]
    local_ref[...] = inverse[...] * (gain_ref[...] * hidden_grad - x * factor[...])
    gain_grad_ref[...] = jnp.sum(hidden_grad * x * inverse[...], axis=0, keepdims=True) * scale


def local_terms(sums, cotangent, x, hidden_grad, gain_row, scale):
    tokens, features = x.shape
    tile = tile_of(features, 512)
    column = lambda c: (0, c)
    whole = lambda c: (0, 0)
    return pl.pallas_call(
        functools.partial(local_kernel, scale, len(sums) - 1),
        grid=(features // tile,),
        in_specs=[pl.BlockSpec((2, tokens), whole)] * len(sums)
        + [
            pl.BlockSpec(cotangent.shape, whole),
            pl.BlockSpec((tokens, tile), column),
            pl.BlockSpec((tokens, tile), column),
            pl.BlockSpec((1, tile), column),
        ],
        out_specs=[
            pl.BlockSpec((tokens, tile), column),
            pl.BlockSpec((1, tile), column),
            pl.BlockSpec(cotangent.shape[::-1], whole),
        ],
        out_shape=[
            jax.ShapeDtypeStruct((tokens, features), jnp.float32),
            jax.ShapeDtypeStruct((1, features), jnp.float32),
            jax.ShapeDtypeStruct(cotangent.shape[::-1], jnp.bfloat16),
        ],
        scratch_shapes=[pltpu.VMEM((tokens, 1), jnp.float32)] * 2,
        compiler_params=PARAMS,
        cost_estimate=pl.CostEstimate(
            flops=8 * x.size, bytes_accessed=4 * cotangent.size + 10 * x.size, transcendentals=0
        ),
    )(*sums, cotangent, x, hidden_grad, gain_row)


def add_kernel(local_ref, received_ref, out_ref):
    out_ref[...] = (local_ref[...] + received_ref[...].astype(jnp.float32)).astype(out_ref.dtype)


def add_rows(local, received):
    height, features = received.shape
    tile = tile_of(height, 32)
    block = pl.BlockSpec((tile, features), lambda r: (r, 0))
    return pl.pallas_call(
        add_kernel,
        grid=(height // tile,),
        in_specs=[block, block],
        out_specs=block,
        out_shape=jax.ShapeDtypeStruct(local.shape, received.dtype),
        compiler_params=PARAMS,
        cost_estimate=pl.CostEstimate(flops=received.size, bytes_accessed=8 * received.size, transcendentals=0),
    )(local, received)


def weight_kernel(groups, *refs):
    scaled_refs, gain_ref, blocks, out_ref = refs[:groups], refs[groups], refs[groups + 1 :], refs[-1]
    tokens = blocks[0].shape[0]
    width = scaled_refs[0].shape[1] // tokens
    total = None
    for at in range(groups * width):
        scaled = scaled_refs[at // width][:, at % width * tokens : (at % width + 1) * tokens]
        term = jnp.dot(scaled, blocks[at][...], preferred_element_type=jnp.float32)
        total = term if total is None else total + term
    out_ref[...] = total * gain_ref[...]


def weight_columns(scaled, held, received, gain_row, start, out):
    tokens, features = held[0].shape
    width = received[0].shape[1]
    rows = scaled[0].shape[0]
    tile = tile_of(width, 512)
    first = start // tile
    whole = lambda c: (0, 0)
    placed = lambda c: (0, first + c)
    here = lambda c: (0, c)
    in_specs = [pl.BlockSpec(part.shape, whole) for part in scaled] + [pl.BlockSpec((1, tile), placed)]
    in_specs += [pl.BlockSpec((tokens, tile), placed)] * len(held)
    in_specs += [pl.BlockSpec((tokens, tile), here)] * len(received)
    args, aliases = [*scaled, gain_row, *held, *received], {}
    if out is not None:
        in_specs.append(pl.BlockSpec(memory_space=pl.ANY))
        aliases = {len(args): 0}
        args.append(out)
    sources = len(held) + len(received)
    return pl.pallas_call(
        functools.partial(weight_kernel, len(scaled)),
        grid=(width // tile,),
        in_specs=in_specs,
        out_specs=pl.BlockSpec((rows, tile), placed),
        out_shape=jax.ShapeDtypeStruct((rows, features), jnp.float32),
        input_output_aliases=aliases,
        compiler_params=PARAMS,
        cost_estimate=pl.CostEstimate(
            flops=2 * sources * tokens * rows * width,
            bytes_accessed=2 * sources * tokens * (rows + width) + 4 * rows * width,
            transcendentals=0,
        ),
    )(*args)


def per_device(inputs, norm_gain, value_weight, value_cotangent, upper_grad):
    replicas = Replicas("dp")
    sections = lax.axis_size("pipe")
    slices = lax.axis_size("tensor")
    x = inputs[0]
    tokens, features = x.shape
    gain_row = norm_gain
    cotangent = value_cotangent[0]
    rows = cotangent.shape[1] // replicas.count
    grad_scale = float(tokens * replicas.count) ** (-0.5)
    far = range(1, replicas.groups)
    near = range(1, replicas.width)

    columns = spans(features, Y_PARTS)
    column_part = lambda c, *gates: (after(x, *gates) if gates else x)[:, columns[c][0] : sum(columns[c])]
    part = column_part(0)
    far_x = [[replicas.send(part, high, 0) for high in far]]
    down = [(i, i - 1) for i in range(1, sections)]
    upper = lax.ppermute(after(upper_grad[0], part), "pipe", down)

    hidden_grad, sums = hidden_grad_and_sums(cotangent, value_weight[0], x, gain_row)
    near_x = [replicas.send(after(x, sums), 0, low) for low in near]
    local, gain_grad, scaled = local_terms(
        [sums] + from_others(sums, "tensor"), cotangent, x, hidden_grad, gain_row, grad_scale
    )

    by_core = scaled.reshape(replicas.count, rows, tokens)
    turn = replicas.width - 1
    rows_for = lambda high, low: lax.dynamic_index_in_dim(by_core, replicas.index(high, low), 0, False)
    pair = [[rows_for(high, turn if high else 0)] for high in range(replicas.groups)]
    for low in near:
        theirs = jnp.stack([rows_for(high, turn + low if high else low) for high in range(replicas.groups)])
        swapped = replicas.send(theirs, 0, low)
        for high in range(replicas.groups):
            pair[high].append(swapped[high])
    pair = [jnp.concatenate(blocks, axis=1) for blocks in pair]
    cots = [pair[0]]
    share = tokens * replicas.width // slices
    mine = lax.axis_index("tensor")
    got = [
        replicas.send(lax.dynamic_slice_in_dim(pair[high], mine * share, share, axis=1), high, turn) for high in far
    ]
    for block in got:
        shares = jnp.concatenate([block] + from_others(block, "tensor"), axis=1)
        pieces = [
            lax.dynamic_slice_in_dim(shares, (mine - at) % slices * share, share, axis=1) for at in range(slices)
        ]
        cots.append(jnp.concatenate(pieces, axis=1))
    gain_far = [replicas.send(gain_grad, high, turn) for high in far]
    gain_grad = sum(gain_far, gain_grad)

    for c in range(1, len(columns)):
        part = column_part(c, *got, *gain_far)
        far_x.append([replicas.send(part, high, 0) for high in far])
    weight_grad = None
    for c, ((start, width), direct) in enumerate(zip(columns, far_x)):
        gates = got + gain_far
        if c == len(columns) - 1:
            input_grad = add_rows(local, upper)
            gated = after(gain_grad, input_grad)
            gain_grad = sum([replicas.send(gated, 0, low) for low in near], gated)
            gates = [gain_grad] + [w for w in [weight_grad] if w is not None]
        received = []
        for block in direct:
            handed = after(block, *gates) if gates else block
            received += [replicas.send(handed, 0, low) for low in near] + [block]
        weight_grad = weight_columns(cots, [x] + near_x, received, gain_row, start, weight_grad)
    return (input_grad[None], weight_grad[None], gain_grad)


def solution(mesh):
    return jax.shard_map(
        per_device,
        mesh=mesh,
        in_specs=(
            P("pipe", "dp", "tensor"),
            P("pipe", "tensor"),
            P("pipe", None, "tensor"),
            P("pipe", "dp", None),
            P("pipe", "dp", "tensor"),
        ),
        out_specs=(P("pipe", "dp", "tensor"), P("pipe", "dp", "tensor"), P("pipe", "tensor")),
        check_vma=False,
    )
```

```python
import functools

import jax
import jax.numpy as jnp
from jax import lax
from jax.experimental import pallas as pl
from jax.experimental.pallas import tpu as pltpu
from jax.sharding import PartitionSpec as P

D = 8192
EPS = 1e-05
Y_PARTS = (5, 3)
MIB = 1 << 20
PARAMS = pltpu.CompilerParams(vmem_limit_bytes=16 * MIB)


def after(value, *others):
    return lax.optimization_barrier((value,) + others)[0]


def spans(total, parts):
    unit = total // sum(parts)
    ends = [unit * sum(parts[: i + 1]) for i in range(len(parts))]
    return list(zip([0] + ends[:-1], [unit * p for p in parts]))


def tile_of(width, largest):
    tile = min(width, largest)
    while width % tile:
        tile //= 2
    return tile


def from_others(array, axis):
    count = lax.axis_size(axis)
    return [lax.ppermute(array, axis, [(i, (i + by) % count) for i in range(count)]) for by in range(1, count)]


class Replicas:
    def __init__(self, axis):
        self.axis = axis
        self.count = lax.axis_size(axis)
        self.width = 2 if self.count % 2 == 0 else 1
        self.groups = self.count // self.width

    def to(self, index, high, low):
        return (index // self.width + high) % self.groups * self.width + (index % self.width + low) % self.width

    def index(self, high, low):
        return self.to(lax.axis_index(self.axis), high, low)

    def send(self, array, high, low):
        return lax.ppermute(array, self.axis, [(i, self.to(i, high, low)) for i in range(self.count)])


def lanes_to_row(sums):
    return jnp.sum(sums.T, axis=0, keepdims=True)


def row_to_column(row):
    return jnp.broadcast_to(row, (128, row.shape[1])).T[:, :1]


def fold_lanes(array):
    total = array[:, :128]
    for at in range(128, array.shape[1], 128):
        total = total + array[:, at : at + 128]
    return total


def inverse_row(sums):
    total = sums[0][...]
    for ref in sums[1:]:
        total = total + ref[...]
    return lax.rsqrt(total / D + EPS)


def scale_kernel(scale, *refs):
    sums, cot_ref, scaled_ref = refs[:-2], refs[-2], refs[-1]
    scaled_ref[...] = (cot_ref[...].astype(jnp.float32).T * (inverse_row(sums) * scale)).astype(jnp.bfloat16)


def scaled_cotangent(sums, cotangent, scale):
    return pl.pallas_call(
        functools.partial(scale_kernel, scale),
        out_shape=jax.ShapeDtypeStruct(cotangent.shape[::-1], jnp.bfloat16),
        compiler_params=PARAMS,
        cost_estimate=pl.CostEstimate(
            flops=2 * cotangent.size, bytes_accessed=4 * cotangent.size, transcendentals=0
        ),
    )(*sums, cotangent)


def grad_kernel(scale, others, *refs):
    sums = refs[: others + 1]
    cot_ref, weight_ref, x_ref, gain_ref, scaled_grad_ref, gain_grad_ref, center_ref = refs[others + 1 : -2]
    inverse, centers = refs[-2:]
    step = pl.program_id(0)

    @pl.when(step == 0)
    def _():
        inverse[...] = row_to_column(inverse_row(sums))
        centers[...] = jnp.zeros_like(centers)

    hidden_grad = jnp.dot(cot_ref[...], weight_ref[...], preferred_element_type=jnp.float32)
    scaled_grad = inverse[...] * hidden_grad
    product = scaled_grad * x_ref[...].astype(jnp.float32)
    gain_grad_ref[...] = jnp.sum(product, axis=0, keepdims=True) * scale
    centers[...] += fold_lanes(gain_ref[...] * product)
    scaled_grad_ref[...] = (gain_ref[...] * scaled_grad).astype(jnp.bfloat16)

    @pl.when(step == pl.num_programs(0) - 1)
    def _():
        center_ref[...] = lanes_to_row(centers[...])


def scaled_grads(sums, cotangent, weight, x, gain_row, scale):
    tokens, features = x.shape
    tile = tile_of(features, 1024)
    column = lambda c: (0, c)
    whole = lambda c: (0, 0)
    return pl.pallas_call(
        functools.partial(grad_kernel, scale, len(sums) - 1),
        grid=(features // tile,),
        in_specs=[pl.BlockSpec((1, tokens), whole)] * len(sums)
        + [
            pl.BlockSpec(cotangent.shape, whole),
            pl.BlockSpec((weight.shape[0], tile), column),
            pl.BlockSpec((tokens, tile), column),
            pl.BlockSpec((1, tile), column),
        ],
        out_specs=[
            pl.BlockSpec((tokens, tile), column),
            pl.BlockSpec((1, tile), column),
            pl.BlockSpec((1, tokens), whole),
        ],
        out_shape=[
            jax.ShapeDtypeStruct((tokens, features), jnp.bfloat16),
            jax.ShapeDtypeStruct((1, features), jnp.float32),
            jax.ShapeDtypeStruct((1, tokens), jnp.float32),
        ],
        scratch_shapes=[pltpu.VMEM((tokens, 1), jnp.float32), pltpu.VMEM((tokens, 128), jnp.float32)],
        compiler_params=PARAMS,
        cost_estimate=pl.CostEstimate(
            flops=2 * tokens * features * weight.shape[0],
            bytes_accessed=2 * (weight.size + cotangent.size + 2 * x.size),
            transcendentals=0,
        ),
    )(*sums, cotangent, weight, x, gain_row)


def add_kernel(others, *refs):
    sums, centers = refs[: others + 1], refs[others + 1 : 2 * others + 2]
    scaled_grad_ref, x_ref, received_ref, out_ref, factor = refs[2 * others + 2 :]

    @pl.when(pl.program_id(0) == 0)
    def _():
        inverse = inverse_row(sums)
        center = centers[0][...]
        for ref in centers[1:]:
            center = center + ref[...]
        factor[...] = row_to_column(inverse * inverse * (center / D))

    height = x_ref.shape[0]
    rows = pl.ds(pl.multiple_of(pl.program_id(0) * height, height), height)
    local = scaled_grad_ref[...].astype(jnp.float32) - x_ref[...].astype(jnp.float32) * factor[rows]
    out_ref[...] = (local + received_ref[...].astype(jnp.float32)).astype(out_ref.dtype)


def add_rows(sums, centers, scaled_grad, x, received):
    tokens, features = received.shape
    tile = tile_of(tokens, 128)
    block = pl.BlockSpec((tile, features), lambda r: (r, 0))
    return pl.pallas_call(
        functools.partial(add_kernel, len(sums) - 1),
        grid=(tokens // tile,),
        in_specs=[pl.BlockSpec((1, tokens), lambda r: (0, 0))] * (2 * len(sums)) + [block] * 3,
        out_specs=block,
        out_shape=jax.ShapeDtypeStruct(x.shape, received.dtype),
        scratch_shapes=[pltpu.VMEM((tokens, 1), jnp.float32)],
        compiler_params=PARAMS,
        cost_estimate=pl.CostEstimate(flops=4 * x.size, bytes_accessed=8 * x.size, transcendentals=0),
    )(*sums, *centers, scaled_grad, x, received)


def weight_kernel(groups, *refs):
    scaled_refs, gain_ref, blocks, out_ref = refs[:groups], refs[groups], refs[groups + 1 :], refs[-1]
    tokens = blocks[0].shape[0]
    width = scaled_refs[0].shape[1] // tokens
    total = None
    for at in range(groups * width):
        scaled = scaled_refs[at // width][:, at % width * tokens : (at % width + 1) * tokens]
        term = jnp.dot(scaled, blocks[at][...], preferred_element_type=jnp.float32)
        total = term if total is None else total + term
    out_ref[...] = total * gain_ref[...]


def weight_columns(scaled, held, received, gain_row, start, out):
    tokens, features = held[0].shape
    width = received[0].shape[1]
    rows = scaled[0].shape[0]
    tile = next(t for t in (1536, 1280, 768, 640, 512, 256, 128) if width % t == 0 and start % t == 0)
    first = start // tile
    whole = lambda c: (0, 0)
    placed = lambda c: (0, first + c)
    here = lambda c: (0, c)
    in_specs = [pl.BlockSpec(part.shape, whole) for part in scaled] + [pl.BlockSpec((1, tile), placed)]
    in_specs += [pl.BlockSpec((tokens, tile), placed)] * len(held)
    in_specs += [pl.BlockSpec((tokens, tile), here)] * len(received)
    args, aliases = [*scaled, gain_row, *held, *received], {}
    if out is not None:
        in_specs.append(pl.BlockSpec(memory_space=pl.ANY))
        aliases = {len(args): 0}
        args.append(out)
    sources = len(held) + len(received)
    return pl.pallas_call(
        functools.partial(weight_kernel, len(scaled)),
        grid=(width // tile,),
        in_specs=in_specs,
        out_specs=pl.BlockSpec((rows, tile), placed),
        out_shape=jax.ShapeDtypeStruct((rows, features), jnp.float32),
        input_output_aliases=aliases,
        compiler_params=PARAMS,
        cost_estimate=pl.CostEstimate(
            flops=2 * sources * tokens * rows * width,
            bytes_accessed=2 * sources * tokens * (rows + width) + 4 * rows * width,
            transcendentals=0,
        ),
    )(*args)


def per_device(inputs, norm_gain, value_weight, value_cotangent, upper_grad):
    replicas = Replicas("dp")
    sections = lax.axis_size("pipe")
    slices = lax.axis_size("tensor")
    x = inputs[0]
    tokens, features = x.shape
    gain_row = norm_gain
    cotangent = value_cotangent[0]
    rows = cotangent.shape[1] // replicas.count
    grad_scale = float(tokens * replicas.count) ** (-0.5)
    far = range(1, replicas.groups)
    near = range(1, replicas.width)

    columns = spans(features, Y_PARTS)
    column_part = lambda c, *gates: (after(x, *gates) if gates else x)[:, columns[c][0] : sum(columns[c])]
    part = column_part(0)
    far_x = [[replicas.send(part, high, 0) for high in far]]
    down = [(i, i - 1) for i in range(1, sections)]
    upper = lax.ppermute(upper_grad[0], "pipe", down)

    squares = jnp.sum(jnp.square(x.astype(jnp.float32)), axis=1)[None]
    sums = [squares] + from_others(squares, "tensor")
    scaled = scaled_cotangent(sums, cotangent, grad_scale)
    scaled_grad, gain_grad, center = scaled_grads(sums, cotangent, value_weight[0], x, gain_row, grad_scale)
    centers = [center] + from_others(center, "tensor")
    near_x = [replicas.send(after(x, scaled), 0, low) for low in near]

    by_core = scaled.reshape(replicas.count, rows, tokens)
    turn = replicas.width - 1
    rows_for = lambda high, low: lax.dynamic_index_in_dim(by_core, replicas.index(high, low), 0, False)
    pair = [[rows_for(high, turn if high else 0)] for high in range(replicas.groups)]
    for low in near:
        theirs = jnp.stack([rows_for(high, turn + low if high else low) for high in range(replicas.groups)])
        swapped = replicas.send(theirs, 0, low)
        for high in range(replicas.groups):
            pair[high].append(swapped[high])
    pair = [jnp.concatenate(blocks, axis=1) for blocks in pair]
    cots = [pair[0]]
    share = tokens * replicas.width // slices
    mine = lax.axis_index("tensor")
    got = [
        replicas.send(lax.dynamic_slice_in_dim(pair[high], mine * share, share, axis=1), high, turn) for high in far
    ]
    for block in got:
        shares = jnp.concatenate([block] + from_others(block, "tensor"), axis=1)
        pieces = [
            lax.dynamic_slice_in_dim(shares, (mine - at) % slices * share, share, axis=1) for at in range(slices)
        ]
        cots.append(jnp.concatenate(pieces, axis=1))
    gain_far = [replicas.send(gain_grad, high, turn) for high in far]
    gain_grad = sum(gain_far, gain_grad)
    gain_grad = sum([replicas.send(gain_grad, 0, low) for low in near], gain_grad)

    for c in range(1, len(columns)):
        part = column_part(c, *got, *gain_far)
        far_x.append([replicas.send(part, high, 0) for high in far])
    weight_grad = None
    for c, ((start, width), direct) in enumerate(zip(columns, far_x)):
        gates = got + gain_far
        if c == len(columns) - 1:
            input_grad = add_rows(sums, centers, scaled_grad, x, upper)
            gates = [input_grad, gain_grad, *cots]
        received = []
        for block in direct:
            handed = after(block, *gates) if gates else block
            received += [replicas.send(handed, 0, low) for low in near] + [block]
        weight_grad = weight_columns(cots, [x] + near_x, received, gain_row, start, weight_grad)
    return (input_grad[None], weight_grad[None], gain_grad)


def solution(mesh):
    return jax.shard_map(
        per_device,
        mesh=mesh,
        in_specs=(
            P("pipe", "dp", "tensor"),
            P("pipe", "tensor"),
            P("pipe", None, "tensor"),
            P("pipe", "dp", None),
            P("pipe", "dp", "tensor"),
        ),
        out_specs=(P("pipe", "dp", "tensor"), P("pipe", "dp", "tensor"), P("pipe", "tensor")),
        check_vma=False,
    )
```

```python
import functools

import jax
import jax.numpy as jnp
from jax import lax
from jax.experimental import pallas as pl
from jax.experimental.pallas import tpu as pltpu
from jax.sharding import PartitionSpec as P

D = 8192
EPS = 1e-05
Y_PARTS = (5, 3)
MIB = 1 << 20
PARAMS = pltpu.CompilerParams(vmem_limit_bytes=16 * MIB)


def after(value, *others):
    return lax.optimization_barrier((value,) + others)[0]


def spans(total, parts):
    unit = total // sum(parts)
    ends = [unit * sum(parts[: i + 1]) for i in range(len(parts))]
    return list(zip([0] + ends[:-1], [unit * p for p in parts]))


def tile_of(width, largest):
    tile = min(width, largest)
    while width % tile:
        tile //= 2
    return tile


def from_others(array, axis):
    count = lax.axis_size(axis)
    return [lax.ppermute(array, axis, [(i, (i + by) % count) for i in range(count)]) for by in range(1, count)]


class Replicas:
    def __init__(self, axis):
        self.axis = axis
        self.count = lax.axis_size(axis)
        self.width = 2 if self.count % 2 == 0 else 1
        self.groups = self.count // self.width

    def to(self, index, high, low):
        return (index // self.width + high) % self.groups * self.width + (index % self.width + low) % self.width

    def index(self, high, low):
        return self.to(lax.axis_index(self.axis), high, low)

    def send(self, array, high, low):
        return lax.ppermute(array, self.axis, [(i, self.to(i, high, low)) for i in range(self.count)])


def lanes_to_row(sums):
    return jnp.sum(sums.T, axis=0, keepdims=True)


def row_to_column(row):
    return jnp.broadcast_to(row, (128, row.shape[1])).T[:, :1]


def fold_lanes(array):
    total = array[:, :128]
    for at in range(128, array.shape[1], 128):
        total = total + array[:, at : at + 128]
    return total


def inverse_row(sums):
    total = sums[0][...]
    for ref in sums[1:]:
        total = total + ref[...]
    return lax.rsqrt(total / D + EPS)


def scale_kernel(scale, *refs):
    sums, cot_ref, scaled_ref = refs[:-2], refs[-2], refs[-1]
    scaled_ref[...] = (cot_ref[...].astype(jnp.float32).T * (inverse_row(sums) * scale)).astype(jnp.bfloat16)


def scaled_cotangent(sums, cotangent, scale):
    return pl.pallas_call(
        functools.partial(scale_kernel, scale),
        out_shape=jax.ShapeDtypeStruct(cotangent.shape[::-1], jnp.bfloat16),
        compiler_params=PARAMS,
        cost_estimate=pl.CostEstimate(flops=1, bytes_accessed=1, transcendentals=0),
    )(*sums, cotangent)


def grad_kernel(scale, others, *refs):
    sums = refs[: others + 1]
    cot_ref, weight_ref, x_ref, gain_ref, scaled_grad_ref, gain_grad_ref, center_ref = refs[others + 1 : -2]
    inverse, centers = refs[-2:]
    step = pl.program_id(0)

    @pl.when(step == 0)
    def _():
        inverse[...] = row_to_column(inverse_row(sums))
        centers[...] = jnp.zeros_like(centers)

    hidden_grad = jnp.dot(cot_ref[...], weight_ref[...], preferred_element_type=jnp.float32)
    scaled_grad = inverse[...] * hidden_grad
    product = scaled_grad * x_ref[...].astype(jnp.float32)
    gain_grad_ref[...] = jnp.sum(product, axis=0, keepdims=True) * scale
    centers[...] += fold_lanes(gain_ref[...] * product)
    scaled_grad_ref[...] = (gain_ref[...] * scaled_grad).astype(jnp.bfloat16)

    @pl.when(step == pl.num_programs(0) - 1)
    def _():
        center_ref[...] = lanes_to_row(centers[...])


def scaled_grads(sums, cotangent, weight, x, gain_row, scale):
    tokens, features = x.shape
    tile = tile_of(features, 1024)
    column = lambda c: (0, c)
    whole = lambda c: (0, 0)
    return pl.pallas_call(
        functools.partial(grad_kernel, scale, len(sums) - 1),
        grid=(features // tile,),
        in_specs=[pl.BlockSpec((1, tokens), whole)] * len(sums)
        + [
            pl.BlockSpec(cotangent.shape, whole),
            pl.BlockSpec((weight.shape[0], tile), column),
            pl.BlockSpec((tokens, tile), column),
            pl.BlockSpec((1, tile), column),
        ],
        out_specs=[
            pl.BlockSpec((tokens, tile), column),
            pl.BlockSpec((1, tile), column),
            pl.BlockSpec((1, tokens), whole),
        ],
        out_shape=[
            jax.ShapeDtypeStruct((tokens, features), jnp.bfloat16),
            jax.ShapeDtypeStruct((1, features), jnp.float32),
            jax.ShapeDtypeStruct((1, tokens), jnp.float32),
        ],
        scratch_shapes=[pltpu.VMEM((tokens, 1), jnp.float32), pltpu.VMEM((tokens, 128), jnp.float32)],
        compiler_params=PARAMS,
        cost_estimate=pl.CostEstimate(flops=1, bytes_accessed=1, transcendentals=0),
    )(*sums, cotangent, weight, x, gain_row)


def local_kernel(others, *refs):
    sums, centers = refs[: others + 1], refs[others + 1 : 2 * others + 2]
    scaled_grad_ref, x_ref, out_ref, factor = refs[2 * others + 2 :]

    @pl.when(pl.program_id(0) == 0)
    def _():
        inverse = inverse_row(sums)
        center = centers[0][...]
        for ref in centers[1:]:
            center = center + ref[...]
        factor[...] = row_to_column(inverse * inverse * (center / D))

    height = x_ref.shape[0]
    rows = pl.ds(pl.multiple_of(pl.program_id(0) * height, height), height)
    local = scaled_grad_ref[...].astype(jnp.float32) - x_ref[...].astype(jnp.float32) * factor[rows]
    out_ref[...] = local.astype(out_ref.dtype)


def local_part(sums, centers, scaled_grad, x):
    tokens, features = x.shape
    tile = tile_of(tokens, 128)
    block = pl.BlockSpec((tile, features), lambda r: (r, 0))
    return pl.pallas_call(
        functools.partial(local_kernel, len(sums) - 1),
        grid=(tokens // tile,),
        in_specs=[pl.BlockSpec((1, tokens), lambda r: (0, 0))] * (2 * len(sums)) + [block] * 2,
        out_specs=block,
        out_shape=jax.ShapeDtypeStruct(x.shape, jnp.bfloat16),
        scratch_shapes=[pltpu.VMEM((tokens, 1), jnp.float32)],
        compiler_params=PARAMS,
        cost_estimate=pl.CostEstimate(flops=1, bytes_accessed=1, transcendentals=0),
    )(*sums, *centers, scaled_grad, x)


def add_kernel(local_ref, received_ref, out_ref):
    out_ref[...] = (local_ref[...].astype(jnp.float32) + received_ref[...].astype(jnp.float32)).astype(out_ref.dtype)


def add_rows(local, received):
    tokens, features = received.shape
    tile = tile_of(tokens, 128)
    block = pl.BlockSpec((tile, features), lambda r: (r, 0))
    return pl.pallas_call(
        add_kernel,
        grid=(tokens // tile,),
        in_specs=[block] * 2,
        out_specs=block,
        out_shape=jax.ShapeDtypeStruct(received.shape, received.dtype),
        compiler_params=PARAMS,
        cost_estimate=pl.CostEstimate(flops=1, bytes_accessed=1, transcendentals=0),
    )(local, received)


def weight_kernel(groups, *refs):
    scaled_refs, gain_ref, blocks, out_ref = refs[:groups], refs[groups], refs[groups + 1 :], refs[-1]
    tokens = blocks[0].shape[0]
    width = scaled_refs[0].shape[1] // tokens
    total = None
    for at in range(groups * width):
        scaled = scaled_refs[at // width][:, at % width * tokens : (at % width + 1) * tokens]
        term = jnp.dot(scaled, blocks[at][...], preferred_element_type=jnp.float32)
        total = term if total is None else total + term
    out_ref[...] = total * gain_ref[...]


def weight_columns(scaled, held, received, gain_row, start, out):
    tokens, features = held[0].shape
    width = received[0].shape[1]
    rows = scaled[0].shape[0]
    tile = next(t for t in (1536, 1280, 768, 640, 512, 256, 128) if width % t == 0 and start % t == 0)
    first = start // tile
    whole = lambda c: (0, 0)
    placed = lambda c: (0, first + c)
    here = lambda c: (0, c)
    in_specs = [pl.BlockSpec(part.shape, whole) for part in scaled] + [pl.BlockSpec((1, tile), placed)]
    in_specs += [pl.BlockSpec((tokens, tile), placed)] * len(held)
    in_specs += [pl.BlockSpec((tokens, tile), here)] * len(received)
    args, aliases = [*scaled, gain_row, *held, *received], {}
    if out is not None:
        in_specs.append(pl.BlockSpec(memory_space=pl.ANY))
        aliases = {len(args): 0}
        args.append(out)
    sources = len(held) + len(received)
    return pl.pallas_call(
        functools.partial(weight_kernel, len(scaled)),
        grid=(width // tile,),
        in_specs=in_specs,
        out_specs=pl.BlockSpec((rows, tile), placed),
        out_shape=jax.ShapeDtypeStruct((rows, features), jnp.float32),
        input_output_aliases=aliases,
        compiler_params=PARAMS,
        cost_estimate=pl.CostEstimate(flops=1, bytes_accessed=1, transcendentals=0),
    )(*args)


def per_device(inputs, norm_gain, value_weight, value_cotangent, upper_grad):
    replicas = Replicas("dp")
    sections = lax.axis_size("pipe")
    slices = lax.axis_size("tensor")
    x = inputs[0]
    tokens, features = x.shape
    gain_row = norm_gain
    cotangent = value_cotangent[0]
    rows = cotangent.shape[1] // replicas.count
    grad_scale = float(tokens * replicas.count) ** (-0.5)
    far = range(1, replicas.groups)
    near = range(1, replicas.width)

    columns = spans(features, Y_PARTS)
    column_part = lambda c, *gates: (after(x, *gates) if gates else x)[:, columns[c][0] : sum(columns[c])]
    part = column_part(0)
    far_x = [[replicas.send(part, high, 0) for high in far]]
    down = [(i, i - 1) for i in range(1, sections)]
    upper = lax.ppermute(upper_grad[0], "pipe", down)

    squares = jnp.sum(jnp.square(x.astype(jnp.float32)), axis=1)[None]
    sums = [squares] + from_others(squares, "tensor")
    scaled = scaled_cotangent(sums, cotangent, grad_scale)
    scaled_grad, gain_grad, center = scaled_grads(sums, cotangent, value_weight[0], x, gain_row, grad_scale)
    centers = [center] + from_others(center, "tensor")
    local = local_part(sums, centers, scaled_grad, x)
    near_x = [replicas.send(after(x, scaled), 0, low) for low in near]

    by_core = scaled.reshape(replicas.count, rows, tokens)
    turn = replicas.width - 1
    rows_for = lambda high, low: lax.dynamic_index_in_dim(by_core, replicas.index(high, low), 0, False)
    pair = [[rows_for(high, turn if high else 0)] for high in range(replicas.groups)]
    for low in near:
        theirs = jnp.stack([rows_for(high, turn + low if high else low) for high in range(replicas.groups)])
        swapped = replicas.send(theirs, 0, low)
        for high in range(replicas.groups):
            pair[high].append(swapped[high])
    pair = [jnp.concatenate(blocks, axis=1) for blocks in pair]
    cots = [pair[0]]
    share = tokens * replicas.width // slices
    mine = lax.axis_index("tensor")
    got = [
        replicas.send(lax.dynamic_slice_in_dim(pair[high], mine * share, share, axis=1), high, turn) for high in far
    ]
    for block in got:
        shares = jnp.concatenate([block] + from_others(block, "tensor"), axis=1)
        pieces = [
            lax.dynamic_slice_in_dim(shares, (mine - at) % slices * share, share, axis=1) for at in range(slices)
        ]
        cots.append(jnp.concatenate(pieces, axis=1))
    gain_far = [replicas.send(after(gain_grad, local), high, turn) for high in far]
    gain_grad = sum(gain_far, gain_grad)
    gain_grad = sum([replicas.send(gain_grad, 0, low) for low in near], gain_grad)

    for c in range(1, len(columns)):
        part = after(column_part(c, center), *got, *gain_far)
        far_x.append([replicas.send(part, high, 0) for high in far])
    weight_grad = None
    for c, ((start, width), direct) in enumerate(zip(columns, far_x)):
        gates = got + gain_far
        if c == len(columns) - 1:
            input_grad = add_rows(local, upper)
            gates = [input_grad, gain_grad, *cots]
        received = []
        for block in direct:
            handed = after(block, *gates) if gates else block
            received += [replicas.send(handed, 0, low) for low in near] + [block]
        weight_grad = weight_columns(cots, [x] + near_x, received, gain_row, start, weight_grad)
    return (input_grad[None], weight_grad[None], gain_grad)


def solution(mesh):
    return jax.shard_map(
        per_device,
        mesh=mesh,
        in_specs=(
            P("pipe", "dp", "tensor"),
            P("pipe", "tensor"),
            P("pipe", None, "tensor"),
            P("pipe", "dp", None),
            P("pipe", "dp", "tensor"),
        ),
        out_specs=(P("pipe", "dp", "tensor"), P("pipe", "dp", "tensor"), P("pipe", "tensor")),
        check_vma=False,
    )
```

```python
import functools

import jax
import jax.numpy as jnp
from jax import lax
from jax.experimental import pallas as pl
from jax.experimental.pallas import tpu as pltpu
from jax.sharding import PartitionSpec as P

D = 8192
EPS = 1e-05
Y_PARTS = (5, 3)
MIB = 1 << 20
PARAMS = pltpu.CompilerParams(vmem_limit_bytes=16 * MIB)


def after(value, *others):
    return lax.optimization_barrier((value,) + others)[0]


def spans(total, parts):
    unit = total // sum(parts)
    ends = [unit * sum(parts[: i + 1]) for i in range(len(parts))]
    return list(zip([0] + ends[:-1], [unit * p for p in parts]))


def tile_of(width, largest):
    tile = min(width, largest)
    while width % tile:
        tile //= 2
    return tile


def from_others(array, axis):
    count = lax.axis_size(axis)
    return [lax.ppermute(array, axis, [(i, (i + by) % count) for i in range(count)]) for by in range(1, count)]


class Replicas:
    def __init__(self, axis):
        self.axis = axis
        self.count = lax.axis_size(axis)
        self.width = 2 if self.count % 2 == 0 else 1
        self.groups = self.count // self.width

    def to(self, index, high, low):
        return (index // self.width + high) % self.groups * self.width + (index % self.width + low) % self.width

    def index(self, high, low):
        return self.to(lax.axis_index(self.axis), high, low)

    def send(self, array, high, low):
        return lax.ppermute(array, self.axis, [(i, self.to(i, high, low)) for i in range(self.count)])


def lanes_to_row(sums):
    return jnp.sum(sums.T, axis=0, keepdims=True)


def row_to_column(row):
    return jnp.broadcast_to(row, (128, row.shape[1])).T[:, :1]


def fold_lanes(array):
    total = array[:, :128]
    for at in range(128, array.shape[1], 128):
        total = total + array[:, at : at + 128]
    return total


def inverse_row(sums):
    total = sums[0][...]
    for ref in sums[1:]:
        total = total + ref[...]
    return lax.rsqrt(total / D + EPS)


def scale_kernel(scale, *refs):
    sums, cot_ref, scaled_ref = refs[:-2], refs[-2], refs[-1]
    scaled_ref[...] = (cot_ref[...].astype(jnp.float32).T * (inverse_row(sums) * scale)).astype(jnp.bfloat16)


def scaled_cotangent(sums, cotangent, scale):
    return pl.pallas_call(
        functools.partial(scale_kernel, scale),
        out_shape=jax.ShapeDtypeStruct(cotangent.shape[::-1], jnp.bfloat16),
        compiler_params=PARAMS,
        cost_estimate=pl.CostEstimate(
            flops=2 * cotangent.size, bytes_accessed=4 * cotangent.size, transcendentals=0
        ),
    )(*sums, cotangent)


def grad_kernel(scale, others, *refs):
    sums = refs[: others + 1]
    cot_ref, weight_ref, x_ref, gain_ref, scaled_grad_ref, gain_grad_ref, center_ref = refs[others + 1 : -2]
    inverse, centers = refs[-2:]
    step = pl.program_id(0)

    @pl.when(step == 0)
    def _():
        inverse[...] = row_to_column(inverse_row(sums))
        centers[...] = jnp.zeros_like(centers)

    hidden_grad = jnp.dot(cot_ref[...], weight_ref[...], preferred_element_type=jnp.float32)
    scaled_grad = inverse[...] * hidden_grad
    product = scaled_grad * x_ref[...].astype(jnp.float32)
    gain_grad_ref[...] = jnp.sum(product, axis=0, keepdims=True) * scale
    centers[...] += fold_lanes(gain_ref[...] * product)
    scaled_grad_ref[...] = (gain_ref[...] * scaled_grad).astype(jnp.bfloat16)

    @pl.when(step == pl.num_programs(0) - 1)
    def _():
        center_ref[...] = lanes_to_row(centers[...])


def scaled_grads(sums, cotangent, weight, x, gain_row, scale):
    tokens, features = x.shape
    tile = tile_of(features, 1024)
    column = lambda c: (0, c)
    whole = lambda c: (0, 0)
    return pl.pallas_call(
        functools.partial(grad_kernel, scale, len(sums) - 1),
        grid=(features // tile,),
        in_specs=[pl.BlockSpec((1, tokens), whole)] * len(sums)
        + [
            pl.BlockSpec(cotangent.shape, whole),
            pl.BlockSpec((weight.shape[0], tile), column),
            pl.BlockSpec((tokens, tile), column),
            pl.BlockSpec((1, tile), column),
        ],
        out_specs=[
            pl.BlockSpec((tokens, tile), column),
            pl.BlockSpec((1, tile), column),
            pl.BlockSpec((1, tokens), whole),
        ],
        out_shape=[
            jax.ShapeDtypeStruct((tokens, features), jnp.bfloat16),
            jax.ShapeDtypeStruct((1, features), jnp.float32),
            jax.ShapeDtypeStruct((1, tokens), jnp.float32),
        ],
        scratch_shapes=[pltpu.VMEM((tokens, 1), jnp.float32), pltpu.VMEM((tokens, 128), jnp.float32)],
        compiler_params=PARAMS,
        cost_estimate=pl.CostEstimate(
            flops=2 * tokens * features * weight.shape[0],
            bytes_accessed=2 * (weight.size + cotangent.size + 2 * x.size),
            transcendentals=0,
        ),
    )(*sums, cotangent, weight, x, gain_row)


def local_kernel(others, *refs):
    sums, centers = refs[: others + 1], refs[others + 1 : 2 * others + 2]
    scaled_grad_ref, x_ref, out_ref, factor = refs[2 * others + 2 :]

    @pl.when(pl.program_id(0) == 0)
    def _():
        inverse = inverse_row(sums)
        center = centers[0][...]
        for ref in centers[1:]:
            center = center + ref[...]
        factor[...] = row_to_column(inverse * inverse * (center / D))

    height = x_ref.shape[0]
    rows = pl.ds(pl.multiple_of(pl.program_id(0) * height, height), height)
    local = scaled_grad_ref[...].astype(jnp.float32) - x_ref[...].astype(jnp.float32) * factor[rows]
    out_ref[...] = local.astype(out_ref.dtype)


def local_part(sums, centers, scaled_grad, x):
    tokens, features = x.shape
    tile = tile_of(tokens, 128)
    block = pl.BlockSpec((tile, features), lambda r: (r, 0))
    return pl.pallas_call(
        functools.partial(local_kernel, len(sums) - 1),
        grid=(tokens // tile,),
        in_specs=[pl.BlockSpec((1, tokens), lambda r: (0, 0))] * (2 * len(sums)) + [block] * 2,
        out_specs=block,
        out_shape=jax.ShapeDtypeStruct(x.shape, jnp.bfloat16),
        scratch_shapes=[pltpu.VMEM((tokens, 1), jnp.float32)],
        compiler_params=PARAMS,
        cost_estimate=pl.CostEstimate(flops=3 * x.size, bytes_accessed=6 * x.size, transcendentals=0),
    )(*sums, *centers, scaled_grad, x)


def add_kernel(local_ref, received_ref, out_ref):
    out_ref[...] = (local_ref[...].astype(jnp.float32) + received_ref[...].astype(jnp.float32)).astype(out_ref.dtype)


def add_rows(local, received):
    tokens, features = received.shape
    tile = tile_of(tokens, 128)
    block = pl.BlockSpec((tile, features), lambda r: (r, 0))
    return pl.pallas_call(
        add_kernel,
        grid=(tokens // tile,),
        in_specs=[block] * 2,
        out_specs=block,
        out_shape=jax.ShapeDtypeStruct(received.shape, received.dtype),
        compiler_params=PARAMS,
        cost_estimate=pl.CostEstimate(flops=received.size, bytes_accessed=6 * received.size, transcendentals=0),
    )(local, received)


def products(scaled_ref, blocks):
    tokens = blocks[0].shape[0]
    total = None
    for at, block in enumerate(blocks):
        scaled = scaled_ref[:, at * tokens : (at + 1) * tokens]
        term = jnp.dot(scaled, block[...], preferred_element_type=jnp.float32)
        total = term if total is None else total + term
    return total


def held_kernel(scaled_ref, *refs):
    refs[-1][...] = products(scaled_ref, refs[:-1]).astype(refs[-1].dtype)


def held_product(scaled, held):
    tokens, features = held[0].shape
    rows = scaled.shape[0]
    tile = tile_of(features, 1024)
    column = lambda c: (0, c)
    return pl.pallas_call(
        held_kernel,
        grid=(features // tile,),
        in_specs=[pl.BlockSpec(scaled.shape, lambda c: (0, 0))]
        + [pl.BlockSpec((tokens, tile), column)] * len(held),
        out_specs=pl.BlockSpec((rows, tile), column),
        out_shape=jax.ShapeDtypeStruct((rows, features), jnp.bfloat16),
        compiler_params=PARAMS,
        cost_estimate=pl.CostEstimate(
            flops=2 * scaled.size * features,
            bytes_accessed=2 * (scaled.size + len(held) * tokens * features + rows * features),
            transcendentals=0,
        ),
    )(scaled, *held)


def weight_kernel(groups, *refs):
    scaled_refs, gain_ref, partial_ref, out_ref = refs[:groups], refs[groups], refs[groups + 1], refs[-1]
    blocks = refs[groups + 2 :]
    total = partial_ref[...].astype(jnp.float32)
    width = scaled_refs[0].shape[1] // blocks[0].shape[0] if groups else 0
    for at, scaled_ref in enumerate(scaled_refs):
        total = total + products(scaled_ref, blocks[at * width : (at + 1) * width])
    out_ref[...] = total * gain_ref[...]


def weight_columns(scaled, partial, received, gain_row, start, width, out):
    rows, features = partial.shape
    tile = next(t for t in (1280, 768, 640, 512, 384, 256, 128) if width % t == 0 and start % t == 0)
    first = start // tile
    whole = lambda c: (0, 0)
    placed = lambda c: (0, first + c)
    here = lambda c: (0, c)
    in_specs = [pl.BlockSpec(part.shape, whole) for part in scaled]
    in_specs += [pl.BlockSpec((1, tile), placed), pl.BlockSpec((rows, tile), placed)]
    in_specs += [pl.BlockSpec((block.shape[0], tile), here) for block in received]
    args, aliases = [*scaled, gain_row, partial, *received], {}
    if out is not None:
        in_specs.append(pl.BlockSpec(memory_space=pl.ANY))
        aliases = {len(args): 0}
        args.append(out)
    tokens = sum(block.shape[0] for block in received)
    return pl.pallas_call(
        functools.partial(weight_kernel, len(scaled)),
        grid=(width // tile,),
        in_specs=in_specs,
        out_specs=pl.BlockSpec((rows, tile), placed),
        out_shape=jax.ShapeDtypeStruct((rows, features), jnp.float32),
        input_output_aliases=aliases,
        compiler_params=PARAMS,
        cost_estimate=pl.CostEstimate(
            flops=2 * tokens * rows * width,
            bytes_accessed=2 * tokens * (rows + width) + 6 * rows * width,
            transcendentals=0,
        ),
    )(*args)


def per_device(inputs, norm_gain, value_weight, value_cotangent, upper_grad):
    replicas = Replicas("dp")
    sections = lax.axis_size("pipe")
    slices = lax.axis_size("tensor")
    x = inputs[0]
    tokens, features = x.shape
    gain_row = norm_gain
    cotangent = value_cotangent[0]
    rows = cotangent.shape[1] // replicas.count
    grad_scale = float(tokens * replicas.count) ** (-0.5)
    far = range(1, replicas.groups)
    near = range(1, replicas.width)

    columns = spans(features, Y_PARTS)
    column_part = lambda c, *gates: (after(x, *gates) if gates else x)[:, columns[c][0] : sum(columns[c])]
    part = column_part(0)
    far_x = [[replicas.send(part, high, 0) for high in far]]
    down = [(i, i - 1) for i in range(1, sections)]
    upper = lax.ppermute(upper_grad[0], "pipe", down)

    squares = jnp.sum(jnp.square(x.astype(jnp.float32)), axis=1)[None]
    sums = [squares] + from_others(squares, "tensor")
    scaled = scaled_cotangent(sums, cotangent, grad_scale)
    scaled_grad, gain_grad, center = scaled_grads(sums, cotangent, value_weight[0], x, gain_row, grad_scale)
    centers = [center] + from_others(center, "tensor")
    local = local_part(sums, centers, scaled_grad, x)
    near_x = [replicas.send(x, 0, low) for low in near]

    by_core = scaled.reshape(replicas.count, rows, tokens)
    turn = replicas.width - 1
    rows_for = lambda high, low: lax.dynamic_index_in_dim(by_core, replicas.index(high, low), 0, False)
    pair = [[rows_for(high, turn if high else 0)] for high in range(replicas.groups)]
    for low in near:
        theirs = jnp.stack([rows_for(high, turn + low if high else low) for high in range(replicas.groups)])
        swapped = replicas.send(theirs, 0, low)
        for high in range(replicas.groups):
            pair[high].append(swapped[high])
    pair = [jnp.concatenate(blocks, axis=1) for blocks in pair]
    cots = [pair[0]]
    share = tokens * replicas.width // slices
    mine = lax.axis_index("tensor")
    got = [
        replicas.send(lax.dynamic_slice_in_dim(pair[high], mine * share, share, axis=1), high, turn) for high in far
    ]
    for block in got:
        shares = jnp.concatenate([block] + from_others(block, "tensor"), axis=1)
        pieces = [
            lax.dynamic_slice_in_dim(shares, (mine - at) % slices * share, share, axis=1) for at in range(slices)
        ]
        cots.append(jnp.concatenate(pieces, axis=1))
    partial = held_product(cots[0], [x] + near_x)
    gain_far = [replicas.send(after(gain_grad, local), high, turn) for high in far]
    gain_grad = sum(gain_far, gain_grad)
    gain_grad = sum([replicas.send(gain_grad, 0, low) for low in near], gain_grad)

    for c in range(1, len(columns)):
        part = after(column_part(c, center), *got, *gain_far, partial)
        far_x.append([replicas.send(part, high, 0) for high in far])
    weight_grad = None
    for c, ((start, width), direct) in enumerate(zip(columns, far_x)):
        gates = got + gain_far
        if c == len(columns) - 1:
            input_grad = add_rows(local, upper)
            gates = [input_grad, gain_grad, *cots]
        received = []
        for block in direct:
            handed = after(block, *gates) if gates else block
            received += [replicas.send(handed, 0, low) for low in near] + [block]
        weight_grad = weight_columns(cots[1:], partial, received, gain_row, start, width, weight_grad)
    return (input_grad[None], weight_grad[None], gain_grad)


def solution(mesh):
    return jax.shard_map(
        per_device,
        mesh=mesh,
        in_specs=(
            P("pipe", "dp", "tensor"),
            P("pipe", "tensor"),
            P("pipe", None, "tensor"),
            P("pipe", "dp", None),
            P("pipe", "dp", "tensor"),
        ),
        out_specs=(P("pipe", "dp", "tensor"), P("pipe", "dp", "tensor"), P("pipe", "tensor")),
        check_vma=False,
    )
```

```python
import functools

import jax
import jax.numpy as jnp
from jax import lax
from jax.experimental import pallas as pl
from jax.experimental.pallas import tpu as pltpu
from jax.sharding import PartitionSpec as P

D = 8192
EPS = 1e-05
Y_PARTS = (5, 3)
MIB = 1 << 20
PARAMS = pltpu.CompilerParams(vmem_limit_bytes=16 * MIB)


def after(value, *others):
    return lax.optimization_barrier((value,) + others)[0]


def spans(total, parts):
    unit = total // sum(parts)
    ends = [unit * sum(parts[: i + 1]) for i in range(len(parts))]
    return list(zip([0] + ends[:-1], [unit * p for p in parts]))


def tile_of(width, largest):
    tile = min(width, largest)
    while width % tile:
        tile //= 2
    return tile


def from_others(array, axis):
    count = lax.axis_size(axis)
    return [lax.ppermute(array, axis, [(i, (i + by) % count) for i in range(count)]) for by in range(1, count)]


class Replicas:
    def __init__(self, axis):
        self.axis = axis
        self.count = lax.axis_size(axis)
        self.width = 2 if self.count % 2 == 0 else 1
        self.groups = self.count // self.width

    def to(self, index, high, low):
        return (index // self.width + high) % self.groups * self.width + (index % self.width + low) % self.width

    def index(self, high, low):
        return self.to(lax.axis_index(self.axis), high, low)

    def send(self, array, high, low):
        return lax.ppermute(array, self.axis, [(i, self.to(i, high, low)) for i in range(self.count)])


def lanes_to_row(sums):
    return jnp.sum(sums.T, axis=0, keepdims=True)


def row_to_column(row):
    return jnp.broadcast_to(row, (128, row.shape[1])).T[:, :1]


def fold_lanes(array):
    total = array[:, :128]
    for at in range(128, array.shape[1], 128):
        total = total + array[:, at : at + 128]
    return total


def inverse_row(sums):
    total = sums[0][...]
    for ref in sums[1:]:
        total = total + ref[...]
    return lax.rsqrt(total / D + EPS)


def scale_kernel(scale, *refs):
    sums, cot_ref, scaled_ref = refs[:-2], refs[-2], refs[-1]
    scaled_ref[...] = (cot_ref[...].astype(jnp.float32).T * (inverse_row(sums) * scale)).astype(jnp.bfloat16)


def scaled_cotangent(sums, cotangent, scale):
    return pl.pallas_call(
        functools.partial(scale_kernel, scale),
        out_shape=jax.ShapeDtypeStruct(cotangent.shape[::-1], jnp.bfloat16),
        compiler_params=PARAMS,
        cost_estimate=pl.CostEstimate(flops=1, bytes_accessed=1, transcendentals=0),
    )(*sums, cotangent)


def grad_kernel(scale, others, *refs):
    sums = refs[: others + 1]
    cot_ref, weight_ref, x_ref, gain_ref, scaled_grad_ref, gain_grad_ref, center_ref = refs[others + 1 : -2]
    inverse, centers = refs[-2:]
    step = pl.program_id(0)

    @pl.when(step == 0)
    def _():
        inverse[...] = row_to_column(inverse_row(sums))
        centers[...] = jnp.zeros_like(centers)

    hidden_grad = jnp.dot(cot_ref[...], weight_ref[...], preferred_element_type=jnp.float32)
    scaled_grad = inverse[...] * hidden_grad
    product = scaled_grad * x_ref[...].astype(jnp.float32)
    gain_grad_ref[...] = jnp.sum(product, axis=0, keepdims=True) * scale
    centers[...] += fold_lanes(gain_ref[...] * product)
    scaled_grad_ref[...] = (gain_ref[...] * scaled_grad).astype(jnp.bfloat16)

    @pl.when(step == pl.num_programs(0) - 1)
    def _():
        center_ref[...] = lanes_to_row(centers[...])


def scaled_grads(sums, cotangent, weight, x, gain_row, scale):
    tokens, features = x.shape
    tile = tile_of(features, 1024)
    column = lambda c: (0, c)
    whole = lambda c: (0, 0)
    return pl.pallas_call(
        functools.partial(grad_kernel, scale, len(sums) - 1),
        grid=(features // tile,),
        in_specs=[pl.BlockSpec((1, tokens), whole)] * len(sums)
        + [
            pl.BlockSpec(cotangent.shape, whole),
            pl.BlockSpec((weight.shape[0], tile), column),
            pl.BlockSpec((tokens, tile), column),
            pl.BlockSpec((1, tile), column),
        ],
        out_specs=[
            pl.BlockSpec((tokens, tile), column),
            pl.BlockSpec((1, tile), column),
            pl.BlockSpec((1, tokens), whole),
        ],
        out_shape=[
            jax.ShapeDtypeStruct((tokens, features), jnp.bfloat16),
            jax.ShapeDtypeStruct((1, features), jnp.float32),
            jax.ShapeDtypeStruct((1, tokens), jnp.float32),
        ],
        scratch_shapes=[pltpu.VMEM((tokens, 1), jnp.float32), pltpu.VMEM((tokens, 128), jnp.float32)],
        compiler_params=PARAMS,
        cost_estimate=pl.CostEstimate(flops=1, bytes_accessed=1, transcendentals=0),
    )(*sums, cotangent, weight, x, gain_row)


def local_kernel(others, *refs):
    sums, centers = refs[: others + 1], refs[others + 1 : 2 * others + 2]
    scaled_grad_ref, x_ref, out_ref, factor = refs[2 * others + 2 :]

    @pl.when(pl.program_id(0) == 0)
    def _():
        inverse = inverse_row(sums)
        center = centers[0][...]
        for ref in centers[1:]:
            center = center + ref[...]
        factor[...] = row_to_column(inverse * inverse * (center / D))

    height = x_ref.shape[0]
    rows = pl.ds(pl.multiple_of(pl.program_id(0) * height, height), height)
    local = scaled_grad_ref[...].astype(jnp.float32) - x_ref[...].astype(jnp.float32) * factor[rows]
    out_ref[...] = local.astype(out_ref.dtype)


def local_part(sums, centers, scaled_grad, x):
    tokens, features = x.shape
    tile = tile_of(tokens, 128)
    block = pl.BlockSpec((tile, features), lambda r: (r, 0))
    return pl.pallas_call(
        functools.partial(local_kernel, len(sums) - 1),
        grid=(tokens // tile,),
        in_specs=[pl.BlockSpec((1, tokens), lambda r: (0, 0))] * (2 * len(sums)) + [block] * 2,
        out_specs=block,
        out_shape=jax.ShapeDtypeStruct(x.shape, jnp.bfloat16),
        scratch_shapes=[pltpu.VMEM((tokens, 1), jnp.float32)],
        compiler_params=PARAMS,
        cost_estimate=pl.CostEstimate(flops=1, bytes_accessed=1, transcendentals=0),
    )(*sums, *centers, scaled_grad, x)


def add_kernel(local_ref, received_ref, out_ref):
    out_ref[...] = (local_ref[...].astype(jnp.float32) + received_ref[...].astype(jnp.float32)).astype(out_ref.dtype)


def add_rows(local, received):
    tokens, features = received.shape
    tile = tile_of(tokens, 128)
    block = pl.BlockSpec((tile, features), lambda r: (r, 0))
    return pl.pallas_call(
        add_kernel,
        grid=(tokens // tile,),
        in_specs=[block] * 2,
        out_specs=block,
        out_shape=jax.ShapeDtypeStruct(received.shape, received.dtype),
        compiler_params=PARAMS,
        cost_estimate=pl.CostEstimate(flops=1, bytes_accessed=1, transcendentals=0),
    )(local, received)


def products(scaled_ref, blocks):
    tokens = blocks[0].shape[0]
    total = None
    for at, block in enumerate(blocks):
        scaled = scaled_ref[:, at * tokens : (at + 1) * tokens]
        term = jnp.dot(scaled, block[...], preferred_element_type=jnp.float32)
        total = term if total is None else total + term
    return total


def held_kernel(scaled_ref, *refs):
    refs[-1][...] = products(scaled_ref, refs[:-1]).astype(refs[-1].dtype)


def held_product(scaled, held):
    tokens, features = held[0].shape
    rows = scaled.shape[0]
    tile = tile_of(features, 1024)
    column = lambda c: (0, c)
    return pl.pallas_call(
        held_kernel,
        grid=(features // tile,),
        in_specs=[pl.BlockSpec(scaled.shape, lambda c: (0, 0))]
        + [pl.BlockSpec((tokens, tile), column)] * len(held),
        out_specs=pl.BlockSpec((rows, tile), column),
        out_shape=jax.ShapeDtypeStruct((rows, features), jnp.bfloat16),
        compiler_params=PARAMS,
        cost_estimate=pl.CostEstimate(flops=1, bytes_accessed=1, transcendentals=0),
    )(scaled, *held)


def weight_kernel(groups, *refs):
    scaled_refs, gain_ref, partial_ref, out_ref = refs[:groups], refs[groups], refs[groups + 1], refs[-1]
    blocks = refs[groups + 2 :]
    total = partial_ref[...].astype(jnp.float32)
    width = scaled_refs[0].shape[1] // blocks[0].shape[0] if groups else 0
    for at, scaled_ref in enumerate(scaled_refs):
        total = total + products(scaled_ref, blocks[at * width : (at + 1) * width])
    out_ref[...] = total * gain_ref[...]


def weight_columns(scaled, partial, received, gain_row, start, width, out):
    rows, features = partial.shape
    tile = next(t for t in (1280, 768, 640, 512, 384, 256, 128) if width % t == 0 and start % t == 0)
    first = start // tile
    whole = lambda c: (0, 0)
    placed = lambda c: (0, first + c)
    here = lambda c: (0, c)
    in_specs = [pl.BlockSpec(part.shape, whole) for part in scaled]
    in_specs += [pl.BlockSpec((1, tile), placed), pl.BlockSpec((rows, tile), placed)]
    in_specs += [pl.BlockSpec((block.shape[0], tile), here) for block in received]
    args, aliases = [*scaled, gain_row, partial, *received], {}
    if out is not None:
        in_specs.append(pl.BlockSpec(memory_space=pl.ANY))
        aliases = {len(args): 0}
        args.append(out)
    tokens = sum(block.shape[0] for block in received)
    return pl.pallas_call(
        functools.partial(weight_kernel, len(scaled)),
        grid=(width // tile,),
        in_specs=in_specs,
        out_specs=pl.BlockSpec((rows, tile), placed),
        out_shape=jax.ShapeDtypeStruct((rows, features), jnp.float32),
        input_output_aliases=aliases,
        compiler_params=PARAMS,
        cost_estimate=pl.CostEstimate(flops=1, bytes_accessed=1, transcendentals=0),
    )(*args)


def per_device(inputs, norm_gain, value_weight, value_cotangent, upper_grad):
    replicas = Replicas("dp")
    sections = lax.axis_size("pipe")
    slices = lax.axis_size("tensor")
    x = inputs[0]
    tokens, features = x.shape
    gain_row = norm_gain
    cotangent = value_cotangent[0]
    rows = cotangent.shape[1] // replicas.count
    grad_scale = float(tokens * replicas.count) ** (-0.5)
    far = range(1, replicas.groups)
    near = range(1, replicas.width)

    columns = spans(features, Y_PARTS)
    column_part = lambda c, *gates: (after(x, *gates) if gates else x)[:, columns[c][0] : sum(columns[c])]
    part = column_part(0)
    far_x = [[replicas.send(part, high, 0) for high in far]]
    down = [(i, i - 1) for i in range(1, sections)]
    upper = lax.ppermute(upper_grad[0], "pipe", down)

    squares = jnp.sum(jnp.square(x.astype(jnp.float32)), axis=1)[None]
    sums = [squares] + from_others(squares, "tensor")
    scaled = scaled_cotangent(sums, cotangent, grad_scale)
    scaled_grad, gain_grad, center = scaled_grads(sums, cotangent, value_weight[0], x, gain_row, grad_scale)
    centers = [center] + from_others(center, "tensor")
    local = local_part(sums, centers, scaled_grad, x)
    near_x = [replicas.send(x, 0, low) for low in near]

    by_core = scaled.reshape(replicas.count, rows, tokens)
    turn = replicas.width - 1
    rows_for = lambda high, low: lax.dynamic_index_in_dim(by_core, replicas.index(high, low), 0, False)
    pair = [[rows_for(high, turn if high else 0)] for high in range(replicas.groups)]
    for low in near:
        theirs = jnp.stack([rows_for(high, turn + low if high else low) for high in range(replicas.groups)])
        swapped = replicas.send(theirs, 0, low)
        for high in range(replicas.groups):
            pair[high].append(swapped[high])
    pair = [jnp.concatenate(blocks, axis=1) for blocks in pair]
    cots = [pair[0]]
    share = tokens * replicas.width // slices
    mine = lax.axis_index("tensor")
    got = [
        replicas.send(lax.dynamic_slice_in_dim(pair[high], mine * share, share, axis=1), high, turn) for high in far
    ]
    for block in got:
        shares = jnp.concatenate([block] + from_others(block, "tensor"), axis=1)
        pieces = [
            lax.dynamic_slice_in_dim(shares, (mine - at) % slices * share, share, axis=1) for at in range(slices)
        ]
        cots.append(jnp.concatenate(pieces, axis=1))
    partial = held_product(cots[0], [x] + near_x)
    gain_far = [replicas.send(after(gain_grad, local), high, turn) for high in far]
    gain_grad = sum(gain_far, gain_grad)
    gain_grad = sum([replicas.send(gain_grad, 0, low) for low in near], gain_grad)

    for c in range(1, len(columns)):
        part = after(column_part(c, center), *got, *gain_far, partial)
        far_x.append([replicas.send(part, high, 0) for high in far])
    weight_grad = None
    for c, ((start, width), direct) in enumerate(zip(columns, far_x)):
        gates = got + gain_far
        if c == len(columns) - 1:
            input_grad = add_rows(local, upper)
            gates = [input_grad, gain_grad, *cots]
        received = []
        for block in direct:
            handed = after(block, *gates) if gates else block
            received += [replicas.send(handed, 0, low) for low in near] + [block]
        weight_grad = weight_columns(cots[1:], partial, received, gain_row, start, width, weight_grad)
    return (input_grad[None], weight_grad[None], gain_grad)


def solution(mesh):
    return jax.shard_map(
        per_device,
        mesh=mesh,
        in_specs=(
            P("pipe", "dp", "tensor"),
            P("pipe", "tensor"),
            P("pipe", None, "tensor"),
            P("pipe", "dp", None),
            P("pipe", "dp", "tensor"),
        ),
        out_specs=(P("pipe", "dp", "tensor"), P("pipe", "dp", "tensor"), P("pipe", "tensor")),
        check_vma=False,
    )
```

```python
import functools

import jax
import jax.numpy as jnp
from jax import lax
from jax.experimental import pallas as pl
from jax.experimental.pallas import tpu as pltpu
from jax.sharding import PartitionSpec as P

D = 8192
EPS = 1e-05
Y_PARTS = (5, 3)
MIB = 1 << 20
PARAMS = pltpu.CompilerParams(vmem_limit_bytes=16 * MIB)


def after(value, *others):
    return lax.optimization_barrier((value,) + others)[0]


def spans(total, parts):
    unit = total // sum(parts)
    ends = [unit * sum(parts[: i + 1]) for i in range(len(parts))]
    return list(zip([0] + ends[:-1], [unit * p for p in parts]))


def tile_of(width, largest):
    tile = min(width, largest)
    while width % tile:
        tile //= 2
    return tile


def from_others(array, axis):
    count = lax.axis_size(axis)
    return [lax.ppermute(array, axis, [(i, (i + by) % count) for i in range(count)]) for by in range(1, count)]


class Replicas:
    def __init__(self, axis):
        self.axis = axis
        self.count = lax.axis_size(axis)
        self.width = 2 if self.count % 2 == 0 else 1
        self.groups = self.count // self.width

    def to(self, index, high, low):
        return (index // self.width + high) % self.groups * self.width + (index % self.width + low) % self.width

    def index(self, high, low):
        return self.to(lax.axis_index(self.axis), high, low)

    def send(self, array, high, low):
        return lax.ppermute(array, self.axis, [(i, self.to(i, high, low)) for i in range(self.count)])


def lanes_to_row(sums):
    return jnp.sum(sums.T, axis=0, keepdims=True)


def row_to_column(row):
    return jnp.broadcast_to(row, (128, row.shape[1])).T[:, :1]


def fold_lanes(array):
    total = array[:, :128]
    for at in range(128, array.shape[1], 128):
        total = total + array[:, at : at + 128]
    return total


def inverse_row(sums):
    total = sums[0][...]
    for ref in sums[1:]:
        total = total + ref[...]
    return lax.rsqrt(total / D + EPS)


def scale_kernel(scale, *refs):
    sums, cot_ref, scaled_ref = refs[:-2], refs[-2], refs[-1]
    scaled_ref[...] = (cot_ref[...].astype(jnp.float32).T * (inverse_row(sums) * scale)).astype(jnp.bfloat16)


def scaled_cotangent(sums, cotangent, scale):
    return pl.pallas_call(
        functools.partial(scale_kernel, scale),
        out_shape=jax.ShapeDtypeStruct(cotangent.shape[::-1], jnp.bfloat16),
        compiler_params=PARAMS,
        cost_estimate=pl.CostEstimate(
            flops=2 * cotangent.size, bytes_accessed=4 * cotangent.size, transcendentals=0
        ),
    )(*sums, cotangent)


def grad_kernel(scale, others, *refs):
    sums = refs[: others + 1]
    cot_ref, weight_ref, x_ref, gain_ref, scaled_grad_ref, gain_grad_ref, center_ref = refs[others + 1 : -2]
    inverse, centers = refs[-2:]
    step = pl.program_id(0)

    @pl.when(step == 0)
    def _():
        inverse[...] = row_to_column(inverse_row(sums))
        centers[...] = jnp.zeros_like(centers)

    hidden_grad = jnp.dot(cot_ref[...], weight_ref[...], preferred_element_type=jnp.float32)
    scaled_grad = inverse[...] * hidden_grad
    product = scaled_grad * x_ref[...].astype(jnp.float32)
    gain_grad_ref[...] = jnp.sum(product, axis=0, keepdims=True) * scale
    centers[...] += fold_lanes(gain_ref[...] * product)
    scaled_grad_ref[...] = (gain_ref[...] * scaled_grad).astype(jnp.bfloat16)

    @pl.when(step == pl.num_programs(0) - 1)
    def _():
        center_ref[...] = lanes_to_row(centers[...])


def scaled_grads(sums, cotangent, weight, x, gain_row, scale):
    tokens, features = x.shape
    tile = tile_of(features, 1024)
    column = lambda c: (0, c)
    whole = lambda c: (0, 0)
    return pl.pallas_call(
        functools.partial(grad_kernel, scale, len(sums) - 1),
        grid=(features // tile,),
        in_specs=[pl.BlockSpec((1, tokens), whole)] * len(sums)
        + [
            pl.BlockSpec(cotangent.shape, whole),
            pl.BlockSpec((weight.shape[0], tile), column),
            pl.BlockSpec((tokens, tile), column),
            pl.BlockSpec((1, tile), column),
        ],
        out_specs=[
            pl.BlockSpec((tokens, tile), column),
            pl.BlockSpec((1, tile), column),
            pl.BlockSpec((1, tokens), whole),
        ],
        out_shape=[
            jax.ShapeDtypeStruct((tokens, features), jnp.bfloat16),
            jax.ShapeDtypeStruct((1, features), jnp.float32),
            jax.ShapeDtypeStruct((1, tokens), jnp.float32),
        ],
        scratch_shapes=[pltpu.VMEM((tokens, 1), jnp.float32), pltpu.VMEM((tokens, 128), jnp.float32)],
        compiler_params=PARAMS,
        cost_estimate=pl.CostEstimate(
            flops=2 * tokens * features * weight.shape[0],
            bytes_accessed=2 * (weight.size + cotangent.size + 2 * x.size),
            transcendentals=0,
        ),
    )(*sums, cotangent, weight, x, gain_row)


def local_kernel(others, *refs):
    sums, centers = refs[: others + 1], refs[others + 1 : 2 * others + 2]
    scaled_grad_ref, x_ref, out_ref, factor = refs[2 * others + 2 :]

    @pl.when(pl.program_id(0) == 0)
    def _():
        inverse = inverse_row(sums)
        center = centers[0][...]
        for ref in centers[1:]:
            center = center + ref[...]
        factor[...] = row_to_column(inverse * inverse * (center / D))

    height = x_ref.shape[0]
    rows = pl.ds(pl.multiple_of(pl.program_id(0) * height, height), height)
    local = scaled_grad_ref[...].astype(jnp.float32) - x_ref[...].astype(jnp.float32) * factor[rows]
    out_ref[...] = local.astype(out_ref.dtype)


def local_part(sums, centers, scaled_grad, x):
    tokens, features = x.shape
    tile = tile_of(tokens, 128)
    block = pl.BlockSpec((tile, features), lambda r: (r, 0))
    return pl.pallas_call(
        functools.partial(local_kernel, len(sums) - 1),
        grid=(tokens // tile,),
        in_specs=[pl.BlockSpec((1, tokens), lambda r: (0, 0))] * (2 * len(sums)) + [block] * 2,
        out_specs=block,
        out_shape=jax.ShapeDtypeStruct(x.shape, jnp.bfloat16),
        scratch_shapes=[pltpu.VMEM((tokens, 1), jnp.float32)],
        compiler_params=PARAMS,
        cost_estimate=pl.CostEstimate(flops=3 * x.size, bytes_accessed=6 * x.size, transcendentals=0),
    )(*sums, *centers, scaled_grad, x)


def add_kernel(local_ref, received_ref, out_ref):
    out_ref[...] = (local_ref[...].astype(jnp.float32) + received_ref[...].astype(jnp.float32)).astype(out_ref.dtype)


def add_rows(local, received):
    tokens, features = received.shape
    tile = tile_of(tokens, 128)
    block = pl.BlockSpec((tile, features), lambda r: (r, 0))
    return pl.pallas_call(
        add_kernel,
        grid=(tokens // tile,),
        in_specs=[block] * 2,
        out_specs=block,
        out_shape=jax.ShapeDtypeStruct(received.shape, received.dtype),
        compiler_params=pltpu.CompilerParams(vmem_limit_bytes=56 * MIB),
        cost_estimate=pl.CostEstimate(flops=received.size, bytes_accessed=6 * received.size, transcendentals=0),
    )(local, received)


def products(scaled_ref, blocks):
    tokens = blocks[0].shape[0]
    total = None
    for at, block in enumerate(blocks):
        scaled = scaled_ref[:, at * tokens : (at + 1) * tokens]
        term = jnp.dot(scaled, block[...], preferred_element_type=jnp.float32)
        total = term if total is None else total + term
    return total


def held_kernel(scaled_ref, *refs):
    refs[-1][...] = products(scaled_ref, refs[:-1]).astype(refs[-1].dtype)


def held_product(scaled, held):
    tokens, features = held[0].shape
    rows = scaled.shape[0]
    tile = tile_of(features, 1024)
    column = lambda c: (0, c)
    return pl.pallas_call(
        held_kernel,
        grid=(features // tile,),
        in_specs=[pl.BlockSpec(scaled.shape, lambda c: (0, 0))]
        + [pl.BlockSpec((tokens, tile), column)] * len(held),
        out_specs=pl.BlockSpec((rows, tile), column),
        out_shape=jax.ShapeDtypeStruct((rows, features), jnp.bfloat16),
        compiler_params=PARAMS,
        cost_estimate=pl.CostEstimate(
            flops=2 * scaled.size * features,
            bytes_accessed=2 * (scaled.size + len(held) * tokens * features + rows * features),
            transcendentals=0,
        ),
    )(scaled, *held)


def weight_kernel(groups, *refs):
    scaled_refs, gain_ref, partial_ref, out_ref = refs[:groups], refs[groups], refs[groups + 1], refs[-1]
    blocks = refs[groups + 2 :]
    total = partial_ref[...].astype(jnp.float32)
    width = scaled_refs[0].shape[1] // blocks[0].shape[0] if groups else 0
    for at, scaled_ref in enumerate(scaled_refs):
        total = total + products(scaled_ref, blocks[at * width : (at + 1) * width])
    out_ref[...] = total * gain_ref[...]


def weight_columns(scaled, partial, received, gain_row, start, width, out):
    rows, features = partial.shape
    tile = next(t for t in (1280, 768, 640, 512, 384, 256, 128) if width % t == 0 and start % t == 0)
    first = start // tile
    whole = lambda c: (0, 0)
    placed = lambda c: (0, first + c)
    here = lambda c: (0, c)
    in_specs = [pl.BlockSpec(part.shape, whole) for part in scaled]
    in_specs += [pl.BlockSpec((1, tile), placed), pl.BlockSpec((rows, tile), placed)]
    in_specs += [pl.BlockSpec((block.shape[0], tile), here) for block in received]
    args, aliases = [*scaled, gain_row, partial, *received], {}
    if out is not None:
        in_specs.append(pl.BlockSpec(memory_space=pl.ANY))
        aliases = {len(args): 0}
        args.append(out)
    tokens = sum(block.shape[0] for block in received)
    return pl.pallas_call(
        functools.partial(weight_kernel, len(scaled)),
        grid=(width // tile,),
        in_specs=in_specs,
        out_specs=pl.BlockSpec((rows, tile), placed),
        out_shape=jax.ShapeDtypeStruct((rows, features), jnp.float32),
        input_output_aliases=aliases,
        compiler_params=PARAMS,
        cost_estimate=pl.CostEstimate(
            flops=2 * tokens * rows * width,
            bytes_accessed=2 * tokens * (rows + width) + 6 * rows * width,
            transcendentals=0,
        ),
    )(*args)


def per_device(inputs, norm_gain, value_weight, value_cotangent, upper_grad):
    replicas = Replicas("dp")
    sections = lax.axis_size("pipe")
    slices = lax.axis_size("tensor")
    x = inputs[0]
    tokens, features = x.shape
    gain_row = norm_gain
    cotangent = value_cotangent[0]
    rows = cotangent.shape[1] // replicas.count
    grad_scale = float(tokens * replicas.count) ** (-0.5)
    far = range(1, replicas.groups)
    near = range(1, replicas.width)

    columns = spans(features, Y_PARTS)
    column_part = lambda c, *gates: (after(x, *gates) if gates else x)[:, columns[c][0] : sum(columns[c])]
    part = column_part(0)
    far_x = [[replicas.send(part, high, 0) for high in far]]
    down = [(i, i - 1) for i in range(1, sections)]
    upper = lax.ppermute(upper_grad[0], "pipe", down)

    squares = jnp.sum(jnp.square(x.astype(jnp.float32)), axis=1)[None]
    sums = [squares] + from_others(squares, "tensor")
    scaled = scaled_cotangent(sums, cotangent, grad_scale)
    scaled_grad, gain_grad, center = scaled_grads(sums, cotangent, value_weight[0], x, gain_row, grad_scale)
    centers = [center] + from_others(center, "tensor")
    local = local_part(sums, centers, scaled_grad, x)
    near_x = [replicas.send(x, 0, low) for low in near]

    by_core = scaled.reshape(replicas.count, rows, tokens)
    turn = replicas.width - 1
    rows_for = lambda high, low: lax.dynamic_index_in_dim(by_core, replicas.index(high, low), 0, False)
    pair = [[rows_for(high, turn if high else 0)] for high in range(replicas.groups)]
    for low in near:
        theirs = jnp.stack([rows_for(high, turn + low if high else low) for high in range(replicas.groups)])
        swapped = replicas.send(theirs, 0, low)
        for high in range(replicas.groups):
            pair[high].append(swapped[high])
    pair = [jnp.concatenate(blocks, axis=1) for blocks in pair]
    cots = [pair[0]]
    share = tokens * replicas.width // slices
    mine = lax.axis_index("tensor")
    got = [
        replicas.send(lax.dynamic_slice_in_dim(pair[high], mine * share, share, axis=1), high, turn) for high in far
    ]
    for block in got:
        shares = jnp.concatenate([block] + from_others(block, "tensor"), axis=1)
        pieces = [
            lax.dynamic_slice_in_dim(shares, (mine - at) % slices * share, share, axis=1) for at in range(slices)
        ]
        cots.append(jnp.concatenate(pieces, axis=1))
    partial = held_product(cots[0], [x] + near_x)
    gain_far = [replicas.send(after(gain_grad, local), high, turn) for high in far]
    gain_grad = sum(gain_far, gain_grad)
    gain_grad = sum([replicas.send(gain_grad, 0, low) for low in near], gain_grad)

    for c in range(1, len(columns)):
        part = after(column_part(c, center), *got, *gain_far, partial)
        far_x.append([replicas.send(part, high, 0) for high in far])
    weight_grad = None
    for c, ((start, width), direct) in enumerate(zip(columns, far_x)):
        gates = got + gain_far
        if c == len(columns) - 1:
            input_grad = add_rows(local, upper)
            gates = [input_grad, gain_grad, *cots]
        received = []
        for block in direct:
            handed = after(block, *gates) if gates else block
            received += [replicas.send(handed, 0, low) for low in near] + [block]
        weight_grad = weight_columns(cots[1:], partial, received, gain_row, start, width, weight_grad)
    return (input_grad[None], weight_grad[None], gain_grad)


def solution(mesh):
    return jax.shard_map(
        per_device,
        mesh=mesh,
        in_specs=(
            P("pipe", "dp", "tensor"),
            P("pipe", "tensor"),
            P("pipe", None, "tensor"),
            P("pipe", "dp", None),
            P("pipe", "dp", "tensor"),
        ),
        out_specs=(P("pipe", "dp", "tensor"), P("pipe", "dp", "tensor"), P("pipe", "tensor")),
        check_vma=False,
    )
```

```python
import functools

import jax
import jax.numpy as jnp
from jax import lax
from jax.experimental import pallas as pl
from jax.experimental.pallas import tpu as pltpu
from jax.sharding import PartitionSpec as P

D = 8192
EPS = 1e-05
Y_PARTS = (5, 3)
MIB = 1 << 20
PARAMS = pltpu.CompilerParams(vmem_limit_bytes=16 * MIB)


def after(value, *others):
    return lax.optimization_barrier((value,) + others)[0]


def spans(total, parts):
    unit = total // sum(parts)
    ends = [unit * sum(parts[: i + 1]) for i in range(len(parts))]
    return list(zip([0] + ends[:-1], [unit * p for p in parts]))


def tile_of(width, largest):
    tile = min(width, largest)
    while width % tile:
        tile //= 2
    return tile


def from_others(array, axis):
    count = lax.axis_size(axis)
    return [lax.ppermute(array, axis, [(i, (i + by) % count) for i in range(count)]) for by in range(1, count)]


class Replicas:
    def __init__(self, axis):
        self.axis = axis
        self.count = lax.axis_size(axis)
        self.width = 2 if self.count % 2 == 0 else 1
        self.groups = self.count // self.width

    def to(self, index, high, low):
        return (index // self.width + high) % self.groups * self.width + (index % self.width + low) % self.width

    def index(self, high, low):
        return self.to(lax.axis_index(self.axis), high, low)

    def send(self, array, high, low):
        return lax.ppermute(array, self.axis, [(i, self.to(i, high, low)) for i in range(self.count)])


def lanes_to_row(sums):
    return jnp.sum(sums.T, axis=0, keepdims=True)


def row_to_column(row):
    return jnp.broadcast_to(row, (128, row.shape[1])).T[:, :1]


def fold_lanes(array):
    total = array[:, :128]
    for at in range(128, array.shape[1], 128):
        total = total + array[:, at : at + 128]
    return total


def inverse_row(sums):
    total = sums[0][...]
    for ref in sums[1:]:
        total = total + ref[...]
    return lax.rsqrt(total / D + EPS)


def scale_kernel(scale, *refs):
    sums, cot_ref, scaled_ref = refs[:-2], refs[-2], refs[-1]
    scaled_ref[...] = (cot_ref[...].astype(jnp.float32).T * (inverse_row(sums) * scale)).astype(jnp.bfloat16)


def scaled_cotangent(sums, cotangent, scale):
    return pl.pallas_call(
        functools.partial(scale_kernel, scale),
        out_shape=jax.ShapeDtypeStruct(cotangent.shape[::-1], jnp.bfloat16),
        compiler_params=PARAMS,
        cost_estimate=pl.CostEstimate(
            flops=2 * cotangent.size, bytes_accessed=4 * cotangent.size, transcendentals=0
        ),
    )(*sums, cotangent)


def grad_kernel(scale, others, *refs):
    sums = refs[: others + 1]
    cot_ref, weight_ref, x_ref, gain_ref, scaled_grad_ref, gain_grad_ref, center_ref = refs[others + 1 : -2]
    inverse, centers = refs[-2:]
    step = pl.program_id(0)

    @pl.when(step == 0)
    def _():
        inverse[...] = row_to_column(inverse_row(sums))
        centers[...] = jnp.zeros_like(centers)

    hidden_grad = jnp.dot(cot_ref[...], weight_ref[...], preferred_element_type=jnp.float32)
    scaled_grad = inverse[...] * hidden_grad
    product = scaled_grad * x_ref[...].astype(jnp.float32)
    gain_grad_ref[...] = jnp.sum(product, axis=0, keepdims=True) * scale
    centers[...] += fold_lanes(gain_ref[...] * product)
    scaled_grad_ref[...] = (gain_ref[...] * scaled_grad).astype(jnp.bfloat16)

    @pl.when(step == pl.num_programs(0) - 1)
    def _():
        center_ref[...] = lanes_to_row(centers[...])


def scaled_grads(sums, cotangent, weight, x, gain_row, scale):
    tokens, features = x.shape
    tile = tile_of(features, 1024)
    column = lambda c: (0, c)
    whole = lambda c: (0, 0)
    return pl.pallas_call(
        functools.partial(grad_kernel, scale, len(sums) - 1),
        grid=(features // tile,),
        in_specs=[pl.BlockSpec((1, tokens), whole)] * len(sums)
        + [
            pl.BlockSpec(cotangent.shape, whole),
            pl.BlockSpec((weight.shape[0], tile), column),
            pl.BlockSpec((tokens, tile), column),
            pl.BlockSpec((1, tile), column),
        ],
        out_specs=[
            pl.BlockSpec((tokens, tile), column),
            pl.BlockSpec((1, tile), column),
            pl.BlockSpec((1, tokens), whole),
        ],
        out_shape=[
            jax.ShapeDtypeStruct((tokens, features), jnp.bfloat16),
            jax.ShapeDtypeStruct((1, features), jnp.float32),
            jax.ShapeDtypeStruct((1, tokens), jnp.float32),
        ],
        scratch_shapes=[pltpu.VMEM((tokens, 1), jnp.float32), pltpu.VMEM((tokens, 128), jnp.float32)],
        compiler_params=PARAMS,
        cost_estimate=pl.CostEstimate(
            flops=2 * tokens * features * weight.shape[0],
            bytes_accessed=2 * (weight.size + cotangent.size + 2 * x.size),
            transcendentals=0,
        ),
    )(*sums, cotangent, weight, x, gain_row)


def local_kernel(others, *refs):
    sums, centers = refs[: others + 1], refs[others + 1 : 2 * others + 2]
    scaled_grad_ref, x_ref, out_ref, factor = refs[2 * others + 2 :]

    @pl.when(pl.program_id(0) == 0)
    def _():
        inverse = inverse_row(sums)
        center = centers[0][...]
        for ref in centers[1:]:
            center = center + ref[...]
        factor[...] = row_to_column(inverse * inverse * (center / D))

    height = x_ref.shape[0]
    rows = pl.ds(pl.multiple_of(pl.program_id(0) * height, height), height)
    local = scaled_grad_ref[...].astype(jnp.float32) - x_ref[...].astype(jnp.float32) * factor[rows]
    out_ref[...] = local.astype(out_ref.dtype)


def local_part(sums, centers, scaled_grad, x):
    tokens, features = x.shape
    tile = tile_of(tokens, 128)
    block = pl.BlockSpec((tile, features), lambda r: (r, 0))
    return pl.pallas_call(
        functools.partial(local_kernel, len(sums) - 1),
        grid=(tokens // tile,),
        in_specs=[pl.BlockSpec((1, tokens), lambda r: (0, 0))] * (2 * len(sums)) + [block] * 2,
        out_specs=block,
        out_shape=jax.ShapeDtypeStruct(x.shape, jnp.bfloat16),
        scratch_shapes=[pltpu.VMEM((tokens, 1), jnp.float32)],
        compiler_params=PARAMS,
        cost_estimate=pl.CostEstimate(flops=3 * x.size, bytes_accessed=6 * x.size, transcendentals=0),
    )(*sums, *centers, scaled_grad, x)


def add_kernel(local_ref, received_ref, out_ref):
    out_ref[...] = (local_ref[...].astype(jnp.float32) + received_ref[...].astype(jnp.float32)).astype(out_ref.dtype)


def add_rows(local, received):
    tokens, features = received.shape
    tile = tile_of(tokens, 64)
    block = pl.BlockSpec((tile, features), lambda r: (r, 0))
    return pl.pallas_call(
        add_kernel,
        grid=(tokens // tile,),
        in_specs=[block] * 2,
        out_specs=block,
        out_shape=jax.ShapeDtypeStruct(received.shape, received.dtype),
        compiler_params=pltpu.CompilerParams(vmem_limit_bytes=56 * MIB),
        cost_estimate=pl.CostEstimate(flops=received.size, bytes_accessed=6 * received.size, transcendentals=0),
    )(local, received)


def products(scaled_ref, blocks):
    tokens = blocks[0].shape[0]
    total = None
    for at, block in enumerate(blocks):
        scaled = scaled_ref[:, at * tokens : (at + 1) * tokens]
        term = jnp.dot(scaled, block[...], preferred_element_type=jnp.float32)
        total = term if total is None else total + term
    return total


def held_kernel(scaled_ref, *refs):
    refs[-1][...] = products(scaled_ref, refs[:-1]).astype(refs[-1].dtype)


def held_product(scaled, held):
    tokens, features = held[0].shape
    rows = scaled.shape[0]
    tile = tile_of(features, 1024)
    column = lambda c: (0, c)
    return pl.pallas_call(
        held_kernel,
        grid=(features // tile,),
        in_specs=[pl.BlockSpec(scaled.shape, lambda c: (0, 0))]
        + [pl.BlockSpec((tokens, tile), column)] * len(held),
        out_specs=pl.BlockSpec((rows, tile), column),
        out_shape=jax.ShapeDtypeStruct((rows, features), jnp.bfloat16),
        compiler_params=PARAMS,
        cost_estimate=pl.CostEstimate(
            flops=2 * scaled.size * features,
            bytes_accessed=2 * (scaled.size + len(held) * tokens * features + rows * features),
            transcendentals=0,
        ),
    )(scaled, *held)


def weight_kernel(groups, *refs):
    scaled_refs, gain_ref, partial_ref, out_ref = refs[:groups], refs[groups], refs[groups + 1], refs[-1]
    blocks = refs[groups + 2 :]
    total = partial_ref[...].astype(jnp.float32)
    width = scaled_refs[0].shape[1] // blocks[0].shape[0] if groups else 0
    for at, scaled_ref in enumerate(scaled_refs):
        total = total + products(scaled_ref, blocks[at * width : (at + 1) * width])
    out_ref[...] = total * gain_ref[...]


def weight_columns(scaled, partial, received, gain_row, start, width, out):
    rows, features = partial.shape
    tile = next(t for t in (1280, 768, 640, 512, 384, 256, 128) if width % t == 0 and start % t == 0)
    first = start // tile
    whole = lambda c: (0, 0)
    placed = lambda c: (0, first + c)
    here = lambda c: (0, c)
    in_specs = [pl.BlockSpec(part.shape, whole) for part in scaled]
    in_specs += [pl.BlockSpec((1, tile), placed), pl.BlockSpec((rows, tile), placed)]
    in_specs += [pl.BlockSpec((block.shape[0], tile), here) for block in received]
    args, aliases = [*scaled, gain_row, partial, *received], {}
    if out is not None:
        in_specs.append(pl.BlockSpec(memory_space=pl.ANY))
        aliases = {len(args): 0}
        args.append(out)
    tokens = sum(block.shape[0] for block in received)
    return pl.pallas_call(
        functools.partial(weight_kernel, len(scaled)),
        grid=(width // tile,),
        in_specs=in_specs,
        out_specs=pl.BlockSpec((rows, tile), placed),
        out_shape=jax.ShapeDtypeStruct((rows, features), jnp.float32),
        input_output_aliases=aliases,
        compiler_params=PARAMS,
        cost_estimate=pl.CostEstimate(
            flops=2 * tokens * rows * width,
            bytes_accessed=2 * tokens * (rows + width) + 6 * rows * width,
            transcendentals=0,
        ),
    )(*args)


def per_device(inputs, norm_gain, value_weight, value_cotangent, upper_grad):
    replicas = Replicas("dp")
    sections = lax.axis_size("pipe")
    slices = lax.axis_size("tensor")
    x = inputs[0]
    tokens, features = x.shape
    gain_row = norm_gain
    cotangent = value_cotangent[0]
    rows = cotangent.shape[1] // replicas.count
    grad_scale = float(tokens * replicas.count) ** (-0.5)
    far = range(1, replicas.groups)
    near = range(1, replicas.width)

    columns = spans(features, Y_PARTS)
    column_part = lambda c, *gates: (after(x, *gates) if gates else x)[:, columns[c][0] : sum(columns[c])]
    part = column_part(0)
    far_x = [[replicas.send(part, high, 0) for high in far]]
    down = [(i, i - 1) for i in range(1, sections)]
    upper = lax.ppermute(upper_grad[0], "pipe", down)

    squares = jnp.sum(jnp.square(x.astype(jnp.float32)), axis=1)[None]
    sums = [squares] + from_others(squares, "tensor")
    scaled = scaled_cotangent(sums, cotangent, grad_scale)
    scaled_grad, gain_grad, center = scaled_grads(sums, cotangent, value_weight[0], x, gain_row, grad_scale)
    centers = [center] + from_others(center, "tensor")
    local = local_part(sums, centers, scaled_grad, x)
    near_x = [replicas.send(x, 0, low) for low in near]

    by_core = scaled.reshape(replicas.count, rows, tokens)
    turn = replicas.width - 1
    rows_for = lambda high, low: lax.dynamic_index_in_dim(by_core, replicas.index(high, low), 0, False)
    pair = [[rows_for(high, turn if high else 0)] for high in range(replicas.groups)]
    for low in near:
        theirs = jnp.stack([rows_for(high, turn + low if high else low) for high in range(replicas.groups)])
        swapped = replicas.send(theirs, 0, low)
        for high in range(replicas.groups):
            pair[high].append(swapped[high])
    pair = [jnp.concatenate(blocks, axis=1) for blocks in pair]
    cots = [pair[0]]
    share = tokens * replicas.width // slices
    mine = lax.axis_index("tensor")
    got = [
        replicas.send(lax.dynamic_slice_in_dim(pair[high], mine * share, share, axis=1), high, turn) for high in far
    ]
    for block in got:
        shares = jnp.concatenate([block] + from_others(block, "tensor"), axis=1)
        pieces = [
            lax.dynamic_slice_in_dim(shares, (mine - at) % slices * share, share, axis=1) for at in range(slices)
        ]
        cots.append(jnp.concatenate(pieces, axis=1))
    partial = held_product(cots[0], [x] + near_x)
    gain_far = [replicas.send(after(gain_grad, local), high, turn) for high in far]
    gain_grad = sum(gain_far, gain_grad)
    gain_grad = sum([replicas.send(gain_grad, 0, low) for low in near], gain_grad)

    for c in range(1, len(columns)):
        part = after(column_part(c, center), *got, *gain_far, partial)
        far_x.append([replicas.send(part, high, 0) for high in far])
    weight_grad = None
    for c, ((start, width), direct) in enumerate(zip(columns, far_x)):
        gates = got + gain_far
        if c == len(columns) - 1:
            input_grad = add_rows(local, upper)
            gates = [input_grad, gain_grad, *cots]
        received = []
        for block in direct:
            handed = after(block, *gates) if gates else block
            received += [replicas.send(handed, 0, low) for low in near] + [block]
        weight_grad = weight_columns(cots[1:], partial, received, gain_row, start, width, weight_grad)
    return (input_grad[None], weight_grad[None], gain_grad)


def solution(mesh):
    return jax.shard_map(
        per_device,
        mesh=mesh,
        in_specs=(
            P("pipe", "dp", "tensor"),
            P("pipe", "tensor"),
            P("pipe", None, "tensor"),
            P("pipe", "dp", None),
            P("pipe", "dp", "tensor"),
        ),
        out_specs=(P("pipe", "dp", "tensor"), P("pipe", "dp", "tensor"), P("pipe", "tensor")),
        check_vma=False,
    )
```

```python
import functools

import jax
import jax.numpy as jnp
from jax import lax
from jax.experimental import pallas as pl
from jax.experimental.pallas import tpu as pltpu
from jax.sharding import PartitionSpec as P

D = 8192
EPS = 1e-05
Y_PARTS = (5, 3)
MIB = 1 << 20
PARAMS = pltpu.CompilerParams(vmem_limit_bytes=16 * MIB)


def after(value, *others):
    return lax.optimization_barrier((value,) + others)[0]


def spans(total, parts):
    unit = total // sum(parts)
    ends = [unit * sum(parts[: i + 1]) for i in range(len(parts))]
    return list(zip([0] + ends[:-1], [unit * p for p in parts]))


def tile_of(width, largest):
    tile = min(width, largest)
    while width % tile:
        tile //= 2
    return tile


def from_others(array, axis):
    count = lax.axis_size(axis)
    return [lax.ppermute(array, axis, [(i, (i + by) % count) for i in range(count)]) for by in range(1, count)]


class Replicas:
    def __init__(self, axis):
        self.axis = axis
        self.count = lax.axis_size(axis)
        self.width = 2 if self.count % 2 == 0 else 1
        self.groups = self.count // self.width

    def to(self, index, high, low):
        return (index // self.width + high) % self.groups * self.width + (index % self.width + low) % self.width

    def index(self, high, low):
        return self.to(lax.axis_index(self.axis), high, low)

    def send(self, array, high, low):
        return lax.ppermute(array, self.axis, [(i, self.to(i, high, low)) for i in range(self.count)])


def lanes_to_row(sums):
    return jnp.sum(sums.T, axis=0, keepdims=True)


def row_to_column(row):
    return jnp.broadcast_to(row, (128, row.shape[1])).T[:, :1]


def fold_lanes(array):
    total = array[:, :128]
    for at in range(128, array.shape[1], 128):
        total = total + array[:, at : at + 128]
    return total


def inverse_row(sums):
    total = sums[0][...]
    for ref in sums[1:]:
        total = total + ref[...]
    return lax.rsqrt(total / D + EPS)


def scale_kernel(scale, *refs):
    sums, cot_ref, scaled_ref = refs[:-2], refs[-2], refs[-1]
    scaled_ref[...] = (cot_ref[...].astype(jnp.float32).T * (inverse_row(sums) * scale)).astype(jnp.bfloat16)


def scaled_cotangent(sums, cotangent, scale):
    return pl.pallas_call(
        functools.partial(scale_kernel, scale),
        out_shape=jax.ShapeDtypeStruct(cotangent.shape[::-1], jnp.bfloat16),
        compiler_params=PARAMS,
        cost_estimate=pl.CostEstimate(
            flops=2 * cotangent.size, bytes_accessed=4 * cotangent.size, transcendentals=0
        ),
    )(*sums, cotangent)


def grad_kernel(scale, others, *refs):
    sums = refs[: others + 1]
    cot_ref, weight_ref, x_ref, gain_ref, scaled_grad_ref, gain_grad_ref, center_ref = refs[others + 1 : -2]
    inverse, centers = refs[-2:]
    step = pl.program_id(0)

    @pl.when(step == 0)
    def _():
        inverse[...] = row_to_column(inverse_row(sums))
        centers[...] = jnp.zeros_like(centers)

    hidden_grad = jnp.dot(cot_ref[...], weight_ref[...], preferred_element_type=jnp.float32)
    scaled_grad = inverse[...] * hidden_grad
    product = scaled_grad * x_ref[...].astype(jnp.float32)
    gain_grad_ref[...] = jnp.sum(product, axis=0, keepdims=True) * scale
    centers[...] += fold_lanes(gain_ref[...] * product)
    scaled_grad_ref[...] = (gain_ref[...] * scaled_grad).astype(jnp.bfloat16)

    @pl.when(step == pl.num_programs(0) - 1)
    def _():
        center_ref[...] = lanes_to_row(centers[...])


def scaled_grads(sums, cotangent, weight, x, gain_row, scale):
    tokens, features = x.shape
    tile = tile_of(features, 1024)
    column = lambda c: (0, c)
    whole = lambda c: (0, 0)
    return pl.pallas_call(
        functools.partial(grad_kernel, scale, len(sums) - 1),
        grid=(features // tile,),
        in_specs=[pl.BlockSpec((1, tokens), whole)] * len(sums)
        + [
            pl.BlockSpec(cotangent.shape, whole),
            pl.BlockSpec((weight.shape[0], tile), column),
            pl.BlockSpec((tokens, tile), column),
            pl.BlockSpec((1, tile), column),
        ],
        out_specs=[
            pl.BlockSpec((tokens, tile), column),
            pl.BlockSpec((1, tile), column),
            pl.BlockSpec((1, tokens), whole),
        ],
        out_shape=[
            jax.ShapeDtypeStruct((tokens, features), jnp.bfloat16),
            jax.ShapeDtypeStruct((1, features), jnp.float32),
            jax.ShapeDtypeStruct((1, tokens), jnp.float32),
        ],
        scratch_shapes=[pltpu.VMEM((tokens, 1), jnp.float32), pltpu.VMEM((tokens, 128), jnp.float32)],
        compiler_params=PARAMS,
        cost_estimate=pl.CostEstimate(
            flops=2 * tokens * features * weight.shape[0],
            bytes_accessed=2 * (weight.size + cotangent.size + 2 * x.size),
            transcendentals=0,
        ),
    )(*sums, cotangent, weight, x, gain_row)


def local_kernel(others, *refs):
    sums, centers = refs[: others + 1], refs[others + 1 : 2 * others + 2]
    scaled_grad_ref, x_ref, out_ref, factor = refs[2 * others + 2 :]

    @pl.when(pl.program_id(0) == 0)
    def _():
        inverse = inverse_row(sums)
        center = centers[0][...]
        for ref in centers[1:]:
            center = center + ref[...]
        factor[...] = row_to_column(inverse * inverse * (center / D))

    height = x_ref.shape[0]
    rows = pl.ds(pl.multiple_of(pl.program_id(0) * height, height), height)
    local = scaled_grad_ref[...].astype(jnp.float32) - x_ref[...].astype(jnp.float32) * factor[rows]
    out_ref[...] = local.astype(out_ref.dtype)


def local_part(sums, centers, scaled_grad, x):
    tokens, features = x.shape
    tile = tile_of(tokens, 128)
    block = pl.BlockSpec((tile, features), lambda r: (r, 0))
    return pl.pallas_call(
        functools.partial(local_kernel, len(sums) - 1),
        grid=(tokens // tile,),
        in_specs=[pl.BlockSpec((1, tokens), lambda r: (0, 0))] * (2 * len(sums)) + [block] * 2,
        out_specs=block,
        out_shape=jax.ShapeDtypeStruct(x.shape, jnp.bfloat16),
        scratch_shapes=[pltpu.VMEM((tokens, 1), jnp.float32)],
        compiler_params=PARAMS,
        cost_estimate=pl.CostEstimate(flops=3 * x.size, bytes_accessed=6 * x.size, transcendentals=0),
    )(*sums, *centers, scaled_grad, x)


def add_kernel(local_ref, received_ref, out_ref):
    out_ref[...] = (local_ref[...].astype(jnp.float32) + received_ref[...].astype(jnp.float32)).astype(out_ref.dtype)


def add_rows(local, received):
    tokens, features = received.shape
    tile = tile_of(tokens, 256)
    block = pl.BlockSpec((tile, features), lambda r: (r, 0))
    return pl.pallas_call(
        add_kernel,
        grid=(tokens // tile,),
        in_specs=[block] * 2,
        out_specs=block,
        out_shape=jax.ShapeDtypeStruct(received.shape, received.dtype),
        compiler_params=pltpu.CompilerParams(vmem_limit_bytes=56 * MIB),
        cost_estimate=pl.CostEstimate(flops=received.size, bytes_accessed=6 * received.size, transcendentals=0),
    )(local, received)


def products(scaled_ref, blocks):
    tokens = blocks[0].shape[0]
    total = None
    for at, block in enumerate(blocks):
        scaled = scaled_ref[:, at * tokens : (at + 1) * tokens]
        term = jnp.dot(scaled, block[...], preferred_element_type=jnp.float32)
        total = term if total is None else total + term
    return total


def held_kernel(scaled_ref, *refs):
    refs[-1][...] = products(scaled_ref, refs[:-1]).astype(refs[-1].dtype)


def held_product(scaled, held):
    tokens, features = held[0].shape
    rows = scaled.shape[0]
    tile = tile_of(features, 1024)
    column = lambda c: (0, c)
    return pl.pallas_call(
        held_kernel,
        grid=(features // tile,),
        in_specs=[pl.BlockSpec(scaled.shape, lambda c: (0, 0))]
        + [pl.BlockSpec((tokens, tile), column)] * len(held),
        out_specs=pl.BlockSpec((rows, tile), column),
        out_shape=jax.ShapeDtypeStruct((rows, features), jnp.bfloat16),
        compiler_params=PARAMS,
        cost_estimate=pl.CostEstimate(
            flops=2 * scaled.size * features,
            bytes_accessed=2 * (scaled.size + len(held) * tokens * features + rows * features),
            transcendentals=0,
        ),
    )(scaled, *held)


def weight_kernel(groups, *refs):
    scaled_refs, gain_ref, partial_ref, out_ref = refs[:groups], refs[groups], refs[groups + 1], refs[-1]
    blocks = refs[groups + 2 :]
    total = partial_ref[...].astype(jnp.float32)
    width = scaled_refs[0].shape[1] // blocks[0].shape[0] if groups else 0
    for at, scaled_ref in enumerate(scaled_refs):
        total = total + products(scaled_ref, blocks[at * width : (at + 1) * width])
    out_ref[...] = total * gain_ref[...]


def weight_columns(scaled, partial, received, gain_row, start, width, out):
    rows, features = partial.shape
    tile = next(t for t in (1280, 768, 640, 512, 384, 256, 128) if width % t == 0 and start % t == 0)
    first = start // tile
    whole = lambda c: (0, 0)
    placed = lambda c: (0, first + c)
    here = lambda c: (0, c)
    in_specs = [pl.BlockSpec(part.shape, whole) for part in scaled]
    in_specs += [pl.BlockSpec((1, tile), placed), pl.BlockSpec((rows, tile), placed)]
    in_specs += [pl.BlockSpec((block.shape[0], tile), here) for block in received]
    args, aliases = [*scaled, gain_row, partial, *received], {}
    if out is not None:
        in_specs.append(pl.BlockSpec(memory_space=pl.ANY))
        aliases = {len(args): 0}
        args.append(out)
    tokens = sum(block.shape[0] for block in received)
    return pl.pallas_call(
        functools.partial(weight_kernel, len(scaled)),
        grid=(width // tile,),
        in_specs=in_specs,
        out_specs=pl.BlockSpec((rows, tile), placed),
        out_shape=jax.ShapeDtypeStruct((rows, features), jnp.float32),
        input_output_aliases=aliases,
        compiler_params=PARAMS,
        cost_estimate=pl.CostEstimate(
            flops=2 * tokens * rows * width,
            bytes_accessed=2 * tokens * (rows + width) + 6 * rows * width,
            transcendentals=0,
        ),
    )(*args)


def per_device(inputs, norm_gain, value_weight, value_cotangent, upper_grad):
    replicas = Replicas("dp")
    sections = lax.axis_size("pipe")
    slices = lax.axis_size("tensor")
    x = inputs[0]
    tokens, features = x.shape
    gain_row = norm_gain
    cotangent = value_cotangent[0]
    rows = cotangent.shape[1] // replicas.count
    grad_scale = float(tokens * replicas.count) ** (-0.5)
    far = range(1, replicas.groups)
    near = range(1, replicas.width)

    columns = spans(features, Y_PARTS)
    column_part = lambda c, *gates: (after(x, *gates) if gates else x)[:, columns[c][0] : sum(columns[c])]
    part = column_part(0)
    far_x = [[replicas.send(part, high, 0) for high in far]]
    down = [(i, i - 1) for i in range(1, sections)]
    upper = lax.ppermute(upper_grad[0], "pipe", down)

    squares = jnp.sum(jnp.square(x.astype(jnp.float32)), axis=1)[None]
    sums = [squares] + from_others(squares, "tensor")
    scaled = scaled_cotangent(sums, cotangent, grad_scale)
    scaled_grad, gain_grad, center = scaled_grads(sums, cotangent, value_weight[0], x, gain_row, grad_scale)
    centers = [center] + from_others(center, "tensor")
    local = local_part(sums, centers, scaled_grad, x)
    near_x = [replicas.send(x, 0, low) for low in near]

    by_core = scaled.reshape(replicas.count, rows, tokens)
    turn = replicas.width - 1
    rows_for = lambda high, low: lax.dynamic_index_in_dim(by_core, replicas.index(high, low), 0, False)
    pair = [[rows_for(high, turn if high else 0)] for high in range(replicas.groups)]
    for low in near:
        theirs = jnp.stack([rows_for(high, turn + low if high else low) for high in range(replicas.groups)])
        swapped = replicas.send(theirs, 0, low)
        for high in range(replicas.groups):
            pair[high].append(swapped[high])
    pair = [jnp.concatenate(blocks, axis=1) for blocks in pair]
    cots = [pair[0]]
    share = tokens * replicas.width // slices
    mine = lax.axis_index("tensor")
    got = [
        replicas.send(lax.dynamic_slice_in_dim(pair[high], mine * share, share, axis=1), high, turn) for high in far
    ]
    for block in got:
        shares = jnp.concatenate([block] + from_others(block, "tensor"), axis=1)
        pieces = [
            lax.dynamic_slice_in_dim(shares, (mine - at) % slices * share, share, axis=1) for at in range(slices)
        ]
        cots.append(jnp.concatenate(pieces, axis=1))
    partial = held_product(cots[0], [x] + near_x)
    gain_far = [replicas.send(after(gain_grad, local), high, turn) for high in far]
    gain_grad = sum(gain_far, gain_grad)
    gain_grad = sum([replicas.send(gain_grad, 0, low) for low in near], gain_grad)

    for c in range(1, len(columns)):
        part = after(column_part(c, center), *got, *gain_far, partial)
        far_x.append([replicas.send(part, high, 0) for high in far])
    weight_grad = None
    for c, ((start, width), direct) in enumerate(zip(columns, far_x)):
        gates = got + gain_far
        if c == len(columns) - 1:
            input_grad = add_rows(local, upper)
            gates = [input_grad, gain_grad, *cots]
        received = []
        for block in direct:
            handed = after(block, *gates) if gates else block
            received += [replicas.send(handed, 0, low) for low in near] + [block]
        weight_grad = weight_columns(cots[1:], partial, received, gain_row, start, width, weight_grad)
    return (input_grad[None], weight_grad[None], gain_grad)


def solution(mesh):
    return jax.shard_map(
        per_device,
        mesh=mesh,
        in_specs=(
            P("pipe", "dp", "tensor"),
            P("pipe", "tensor"),
            P("pipe", None, "tensor"),
            P("pipe", "dp", None),
            P("pipe", "dp", "tensor"),
        ),
        out_specs=(P("pipe", "dp", "tensor"), P("pipe", "dp", "tensor"), P("pipe", "tensor")),
        check_vma=False,
    )
```
